32 devices in a mesh: fsdp: 8 (over y, x, core), tp: 4 (over z).
Axes of the slice: x: 2, y: 2, z: 4, core: 2. Of those that a mesh axis runs over, the one named last changes fastest.
Arguments:
- tokens: bfloat16 [1024, 4096], P('fsdp'), may hold values from -6 to 6
- gate_packed: bfloat16 [4096, 7680], P('fsdp', 'tp'), may hold values from -0.125 to 0.125
- up_packed: bfloat16 [4096, 7680], P('fsdp', 'tp'), may hold values from -0.125 to 0.125
- col_slots: int32 [32, 60], P(None, 'tp'), may hold values from 0 to 29, as said below
- readout: bfloat16 [15360], P('tp'), may hold values from -0.046875 to 0.046875
- base_logp: float32 [1024], P('fsdp'), may hold values from -4 to 0
- ref_logp: float32 [1024], P('fsdp'), may hold values from -4 to 0
- seq_lengths: int32 [8, 4], P('fsdp'), may hold values from 1 to 64, 128 in all within a row
- pair_index: int32 [16, 2], P('fsdp'), may hold values from 0 to 31, as said below
- noise_flags: int32 [16], P('fsdp'), may hold values 0 or 1
Outputs:
- hidden: bfloat16 [1024, 15360], P('fsdp', 'tp')
- pair_loss: float32 [16], P('fsdp')
The draws below stay inside these ranges and needn't reach their ends.
Inputs may be any that keep to these rules, and one draw needn't show every extreme that they name: `col_slots`: within each block row and tp shard the 15 entries are distinct and increasing, below 30. `seq_lengths`: each fsdp index's 4 lengths sum to 128. `pair_index`: every sequence number appears exactly once.
All inputs are finite; a program needn't handle non-finite values. No bound on the sum of `noise_flags` on one device may be relied on, other than what follows from the above.
Results may differ from the reference program's by a relative error of at most 0.0014.
Values may be sent and summed in bfloat16 or wider, within the bound.
No kernel may reach another device: no remote copies, remote signals or barrier semaphores. Data moves between devices by JAX's collectives and lax.ppermute only.
A program may use at most 128 MiB of HBM per device.

```python
import math
import jax
import jax.numpy as jnp
import numpy as np
from jax import lax

D = 4096
FF = 15360
BLK = 128
TOK_DEV = 128
SEQ_DEV = 4
TOKENS = 1024
NSEQ = 32
PAIRS = 16
SLOTS = 15
N_FSDP = 8
N_TP = 4


def distinct_scores(key, shape, count_last):
    raw_scores = jax.random.randint(key, shape, 0, 1 << 20, dtype=jnp.int32)
    return raw_scores * count_last + jnp.arange(count_last, dtype=jnp.int32)


def draw_col_slots(key, part):
    tp_count = FF // (2 * BLK * SLOTS)
    shape = (D // BLK, tp_count, 2 * SLOTS)
    scores = distinct_scores(jax.random.fold_in(key, 11), shape, 2 * SLOTS)
    ordering = jnp.argsort(scores, axis=-1).astype(jnp.int32)
    picked = jnp.sort(ordering[..., :SLOTS], axis=-1)
    return picked.reshape(D // BLK, tp_count * SLOTS).astype(jnp.int32)


def draw_pair_index(key, part):
    scores = distinct_scores(jax.random.fold_in(key, 23), (NSEQ,), NSEQ)
    seq_order = jnp.argsort(scores).astype(jnp.int32)
    return seq_order.reshape(PAIRS, 2)


def set_ends(entries, stream_key, smallest, top_value):
    spot = [jax.random.randint(jax.random.fold_in(stream_key, axis), (), 0, length) for axis, length in enumerate(entries.shape)]
    widest = entries.shape.index(max(entries.shape))
    beside = spot[:widest] + [(spot[widest] + 1) % entries.shape[widest]] + spot[widest + 1:]
    return entries.at[tuple(spot)].set(smallest).at[tuple(beside)].set(top_value)


def levels(key, dims, pieces, low, high):
    level, own = 1.0, jax.random.fold_in(key, 6)
    for axis_at, blocks in pieces:
        steps = jnp.exp(jax.random.uniform(jax.random.fold_in(own, axis_at), (blocks,), jnp.float32, low / len(pieces), high / len(pieces)))
        level = level * jnp.repeat(steps, dims[axis_at] // blocks).reshape([-1 if axis == axis_at else 1 for axis in range(len(dims))])
    return level


def length_profile(number_of, total, limit, skew):
    portions = [(1 << 20) // math.isqrt(rank ** skew) + 1 for rank in range(2, number_of + 1)]
    rest, given = total - limit - (number_of - 1), [1] * (number_of - 1)
    while rest > 0:
        movable = [i for i in range(number_of - 1) if given[i] < limit]
        mass, budget = sum([portions[i] for i in movable]), rest
        for i in movable:
            extra = min(limit - given[i], max(1, budget * portions[i] // mass), rest)
            given[i] = given[i] + extra
            rest = rest - extra
    return np.array([limit] + given)


def ragged_sizes(stream_key, number_of, total, reach, skew):
    if number_of == 2:
        one = jax.random.randint(stream_key, (), max(1, total - reach), min(reach, total - 1) + 1)
        return jnp.stack([one, total - one])
    sizes = jnp.asarray(length_profile(number_of, total, reach, skew), jnp.int32)
    couples = (number_of - 1) // 2
    donor, taker = sizes[1:1 + 2 * couples:2], sizes[2:2 + 2 * couples:2]
    room = jnp.minimum(donor - 1, reach - taker)
    shifted = jax.random.randint(jax.random.fold_in(stream_key, 1), (couples,), 0, 1 << 20) % (room + 1)
    sizes = sizes.at[1:1 + 2 * couples:2].set(donor - shifted).at[2:2 + 2 * couples:2].set(taker + shifted)
    return sizes[jax.random.permutation(jax.random.fold_in(stream_key, 2), number_of)]


def bell_draw(own_key, extent, width, reach, pieces=(), kind=jnp.bfloat16):
    values = width * jax.random.normal(own_key, extent, jnp.float32)
    if pieces:
        values = values * levels(own_key, extent, pieces, -0.22, 0.18)
    return jnp.clip(values, -reach, reach).astype(kind)


def setup_inputs(seed: int = 0) -> dict:
    key_of = jax.random.split(jax.random.key(seed), 11)
    tokens = bell_draw(key_of[0], (TOKENS, D), 1.0, 6.0, ((0, 8),))
    gate_packed = bell_draw(key_of[1], (D, FF // 2), (D // 2) ** -0.5, 0.125, ((0, 8), (1, 4)))
    up_packed = bell_draw(key_of[2], (D, FF // 2), (D // 2) ** -0.5, 0.125, ((0, 8), (1, 4)))
    col_slots = draw_col_slots(jax.random.fold_in(key_of[10], 71), 0)
    readout = bell_draw(key_of[4], (FF,), FF ** -0.5, 0.046875, ((0, 4),))
    base_logp = jnp.clip(-4.0 + 4.0 * jax.random.uniform(key_of[5], (TOKENS,), jnp.float32) ** levels(key_of[5], (TOKENS,), ((0, 8),), -0.2, 0.2), -4.0, 0.0)
    ref_logp = jnp.clip(-4.0 + 4.0 * jax.random.uniform(key_of[6], (TOKENS,), jnp.float32) ** levels(key_of[6], (TOKENS,), ((0, 8),), -0.2, 0.2), -4.0, 0.0)
    seq_lengths = jax.vmap(lambda own: ragged_sizes(own, SEQ_DEV, TOK_DEV, TOK_DEV // 2, 2))(jax.random.split(key_of[7], N_FSDP)).reshape((N_FSDP, SEQ_DEV)).astype(jnp.int32)
    pair_index = draw_pair_index(jax.random.fold_in(key_of[10], 71), 0)
    noise_flags = set_ends((jax.random.randint(key_of[9], (PAIRS,), 0, 4) < 1).astype(jnp.int32), jax.random.fold_in(key_of[9], 1), 0, 1)
    return {"tokens": tokens, "gate_packed": gate_packed, "up_packed": up_packed, "col_slots": col_slots, "readout": readout, "base_logp": base_logp, "ref_logp": ref_logp, "seq_lengths": seq_lengths, "pair_index": pair_index, "noise_flags": noise_flags}


beta_scale = 0.1
smooth_rate = 0.1


def group_terms(token_group, gate_packed, up_packed, placement, readout):
    tok_rows = token_group.shape[0]

    def block_step(totals, block_row):
        gate_sum, up_sum = totals
        first_row = (block_row * BLK).astype(jnp.int32)
        token_cols = lax.dynamic_slice_in_dim(token_group, first_row, BLK, 1)
        gate_rows = lax.dynamic_slice_in_dim(gate_packed, first_row, BLK, 0)
        up_rows = lax.dynamic_slice_in_dim(up_packed, first_row, BLK, 0)
        row_place = lax.dynamic_index_in_dim(placement, block_row, 0, keepdims=False)
        gate_part = jnp.dot(token_cols, gate_rows, preferred_element_type=jnp.float32).reshape(tok_rows, N_TP, SLOTS, BLK)
        up_part = jnp.dot(token_cols, up_rows, preferred_element_type=jnp.float32).reshape(tok_rows, N_TP, SLOTS, BLK)
        gate_sum = gate_sum + jnp.einsum("xtjc,tjm->xtmc", gate_part, row_place, precision=lax.Precision.HIGHEST)
        up_sum = up_sum + jnp.einsum("xtjc,tjm->xtmc", up_part, row_place, precision=lax.Precision.HIGHEST)
        return (gate_sum, up_sum), None

    empty_acc = jnp.zeros((tok_rows, N_TP, 2 * SLOTS, BLK), jnp.float32)
    block_ids = jnp.arange(D // BLK, dtype=jnp.int32)
    (gate_sum, up_sum), unused = lax.scan(block_step, (empty_acc, empty_acc), block_ids)
    gate_full = gate_sum.reshape(tok_rows, FF)
    up_full = up_sum.reshape(tok_rows, FF)
    hidden = (jax.nn.silu(gate_full) * up_full).astype(jnp.bfloat16)
    contrib = jnp.dot(hidden, readout, preferred_element_type=jnp.float32)
    return hidden, contrib


def reference(tokens, gate_packed, up_packed, col_slots, readout, base_logp, ref_logp, seq_lengths, pair_index, noise_flags):
    column_ids = jnp.arange(2 * SLOTS, dtype=jnp.int32)
    placement = (col_slots.reshape(D // BLK, N_TP, SLOTS)[..., None] == column_ids).astype(jnp.float32)

    def per_group(token_group):
        return group_terms(token_group, gate_packed, up_packed, placement, readout)

    hidden, contrib = lax.map(per_group, tokens.reshape(N_FSDP, TOK_DEV, D))
    hidden = hidden.reshape(TOK_DEV * N_FSDP, FF)
    token_term = ((base_logp - ref_logp) + contrib.reshape(-1)).reshape(N_FSDP, TOK_DEV)
    seq_ends = jnp.cumsum(seq_lengths, axis=1)
    seq_starts = seq_ends - seq_lengths
    positions = jnp.arange(TOK_DEV, dtype=jnp.int32)
    member = (positions[None, None, :] >= seq_starts[:, :, None]) & (positions[None, None, :] < seq_ends[:, :, None])
    seq_ratio = jnp.sum(jnp.where(member, token_term[:, None, :], jnp.float32(0.0)), axis=2).reshape(-1)
    chosen = seq_ratio[pair_index[:, 0]]
    rejected = seq_ratio[pair_index[:, 1]]
    sign_flip = 1.0 - 2.0 * noise_flags.astype(jnp.float32)
    margin = beta_scale * sign_flip * (chosen - rejected)
    pair_loss = -(1.0 - smooth_rate) * jax.nn.log_sigmoid(margin) - smooth_rate * jax.nn.log_sigmoid(-margin)
    return hidden, pair_loss
```

```python
import functools

import jax
import jax.numpy as jnp
from jax import lax
from jax.experimental import pallas as pl
from jax.experimental.pallas import tpu as pltpu
from jax.sharding import PartitionSpec as P

BLK = 128
CORE, X, Y = 1, 2, 4


beta_scale = 0.1
smooth_rate = 0.1


def swap(value, mask):
    return lax.ppermute(value, "fsdp", [(i, i ^ mask) for i in range(8)])


def slot_map(col_slots):
    slots = col_slots.shape[1]
    columns = jnp.arange(2 * slots, dtype=jnp.int32)
    hit = col_slots[:, :, None] == columns[None, None, :]
    number = jnp.arange(1, slots + 1, dtype=jnp.int32)[None, :, None]
    return jnp.sum(jnp.where(hit, number, 0), axis=1) - 1


def partial_kernel(chunks_ref, near_ref, slots_ref, own_tok, near_tok, *refs):
    sources, (own_out, near_out, panel, dense) = refs[:4], refs[4:]
    tokens, depth = own_tok.shape[0], sources[0].shape[0]
    rows = depth // BLK
    for s in range(4):
        own_at = pl.multiple_of(chunks_ref[s] * depth, depth)
        near_at = pl.multiple_of(near_ref[s] * depth, depth)
        panel[:tokens, s * depth : (s + 1) * depth] = own_tok[:, pl.ds(own_at, depth)]
        panel[tokens:, s * depth : (s + 1) * depth] = near_tok[:, pl.ds(near_at, depth)]

    @pl.loop(0, own_out.shape[1] // (2 * BLK))
    def _(pair):
        total = jnp.zeros((2 * tokens, 2 * BLK), jnp.float32)
        for s in range(4):
            for r in range(rows):
                for h in range(2):
                    slot = slots_ref[chunks_ref[s] * rows + r, 2 * pair + h]
                    at = pl.multiple_of(jnp.maximum(slot, 0) * BLK, BLK)
                    block = sources[s][r * BLK : (r + 1) * BLK, pl.ds(at, BLK)]
                    dense[s, r * BLK : (r + 1) * BLK, h * BLK : (h + 1) * BLK] = jnp.where(
                        slot >= 0, block, jnp.zeros_like(block)
                    )
            total += jnp.dot(
                panel[:, s * depth : (s + 1) * depth], dense[s], preferred_element_type=jnp.float32
            )
        at = pl.ds(pl.multiple_of(pair * 2 * BLK, 2 * BLK), 2 * BLK)
        own_out[:, at] = total[:tokens]
        near_out[:, at] = total[tokens:]


def partial_sums(chunks, near, slots, own_tok, near_tok, sources):
    tokens, depth = own_tok.shape[0], sources[0].shape[0]
    width = slots.shape[1] * BLK
    smem, vmem = pl.BlockSpec(memory_space=pltpu.SMEM), pl.BlockSpec(memory_space=pltpu.VMEM)
    out = jax.ShapeDtypeStruct((tokens, width), jnp.float32)
    return pl.pallas_call(
        partial_kernel,
        out_shape=(out, out),
        in_specs=[smem] * 3 + [vmem] * 6,
        out_specs=(vmem, vmem),
        scratch_shapes=[
            pltpu.VMEM((2 * tokens, 4 * depth), jnp.bfloat16),
            pltpu.VMEM((4, depth, 2 * BLK), jnp.bfloat16),
        ],
        compiler_params=pltpu.CompilerParams(vmem_limit_bytes=40 << 20),
        cost_estimate=pl.CostEstimate(
            flops=2 * 2 * tokens * 4 * depth * width,
            bytes_accessed=4 * depth * width + 2 * tokens * width * 4,
            transcendentals=0,
        ),
    )(chunks, near, slots, own_tok, near_tok, *sources)


def pair_losses(token_terms, seq_lengths, pair_index, noise_flags):
    lengths = seq_lengths[0]
    seq_ends = jnp.cumsum(lengths)
    seq_starts = seq_ends - lengths
    positions = jnp.arange(token_terms.shape[0], dtype=jnp.int32)
    member = (positions[None, :] >= seq_starts[:, None]) & (positions[None, :] < seq_ends[:, None])
    share = jnp.sum(jnp.where(member, token_terms[None, :], jnp.float32(0.0)), axis=1)
    n_fsdp, n_tp = lax.axis_size("fsdp"), lax.axis_size("tp")
    spread = jnp.broadcast_to(share, (n_fsdp * n_tp, share.shape[0]))
    shares = lax.all_to_all(spread, ("fsdp", "tp"), 0, 0, tiled=True)
    ratios = jnp.sum(shares.reshape(n_fsdp, n_tp, share.shape[0]), axis=1).reshape(-1)
    seq_ids = jnp.arange(ratios.shape[0], dtype=jnp.int32)
    picked = jnp.sum(
        jnp.where(pair_index[:, :, None] == seq_ids, ratios, jnp.float32(0.0)), axis=2
    )
    sign_flip = 1.0 - 2.0 * noise_flags.astype(jnp.float32)
    margin = beta_scale * sign_flip * (picked[:, 0] - picked[:, 1])
    return -(1.0 - smooth_rate) * jax.nn.log_sigmoid(margin) - smooth_rate * jax.nn.log_sigmoid(
        -margin
    )


def gathered_sums(tokens, gate_packed, up_packed, col_slots):
    slot_count, row_count = col_slots.shape[1], col_slots.shape[0]
    column_ids = jnp.arange(2 * slot_count, dtype=jnp.int32)
    place = (col_slots[:, :, None] == column_ids[None, None, :]).astype(jnp.bfloat16)

    def product(packed):
        whole = lax.all_gather(packed, "fsdp", axis=0, tiled=True)
        blocks = whole.reshape(row_count, BLK, slot_count, BLK)
        dense = jnp.einsum("rnjc,rjm->rnmc", blocks, place, preferred_element_type=jnp.bfloat16)
        dense = dense.reshape(row_count * BLK, 2 * slot_count * BLK)
        return jnp.dot(tokens, dense, preferred_element_type=jnp.float32)

    return product(gate_packed), product(up_packed)


def exchanged_sums(tokens, gate_packed, up_packed, col_slots):
    me = lax.axis_index("fsdp")
    x_at, y_at = (me >> 1) & 1, (me >> 2) & 1
    count = tokens.shape[0]
    quarters = tokens.reshape(count, 2, 2, -1)
    half = tokens.shape[1] // 2
    to_y = lax.dynamic_index_in_dim(quarters, 1 - y_at, 1, keepdims=False).reshape(count, half)
    to_x = lax.dynamic_index_in_dim(quarters, 1 - x_at, 2, keepdims=False).reshape(count, half)
    from_y, from_x = swap(to_y, Y), swap(to_x, X)
    gate_x, up_y = swap(gate_packed, X), swap(up_packed, Y)
    gate_sources = (gate_packed, swap(gate_packed, CORE), gate_x, swap(gate_x, CORE))
    up_sources = (up_packed, swap(up_packed, CORE), up_y, swap(up_y, CORE))
    slots = slot_map(col_slots)
    gate_chunks = me ^ jnp.array([0, CORE, X, X | CORE], jnp.int32)
    up_chunks = me ^ jnp.array([0, CORE, Y, Y | CORE], jnp.int32)
    gate_near = gate_chunks & 3
    up_near = ((up_chunks >> 1) & 2) | (up_chunks & 1)
    gate_own, gate_other = partial_sums(gate_chunks, gate_near, slots, tokens, from_y, gate_sources)
    up_own, up_other = partial_sums(up_chunks, up_near, slots, tokens, from_x, up_sources)
    gate_in = swap(gate_other.astype(jnp.float16), Y)
    up_in = swap(up_other.astype(jnp.float16), X)
    return gate_own + gate_in.astype(jnp.float32), up_own + up_in.astype(jnp.float32)


def shards(
    tokens,
    gate_packed,
    up_packed,
    col_slots,
    readout,
    base_logp,
    ref_logp,
    seq_lengths,
    pair_index,
    noise_flags,
):
    whole_blocks = gate_packed.shape[0] % BLK == 0
    sums = exchanged_sums if lax.axis_size("fsdp") == 8 and whole_blocks else gathered_sums
    gate_sum, up_sum = sums(tokens, gate_packed, up_packed, col_slots)
    hidden = (jax.nn.silu(gate_sum) * up_sum).astype(jnp.bfloat16)
    contrib = jnp.dot(hidden, readout, preferred_element_type=jnp.float32)
    local_term = jnp.where(lax.axis_index("tp") == 0, base_logp - ref_logp, jnp.float32(0.0))
    return hidden, pair_losses(local_term + contrib, seq_lengths, pair_index, noise_flags)


def solution(mesh):
    in_specs = (
        P("fsdp", None),
        P("fsdp", "tp"),
        P("fsdp", "tp"),
        P(None, "tp"),
        P("tp"),
        P("fsdp"),
        P("fsdp"),
        P("fsdp", None),
        P("fsdp", None),
        P("fsdp"),
    )
    out_specs = (P("fsdp", "tp"), P("fsdp"))
    return jax.shard_map(shards, mesh=mesh, in_specs=in_specs, out_specs=out_specs, check_vma=False)
```

```python
import functools

import jax
import jax.numpy as jnp
from jax import lax
from jax.experimental import pallas as pl
from jax.experimental.pallas import tpu as pltpu
from jax.sharding import PartitionSpec as P

BLK = 128
EARLY_VMEM, LATE_VMEM = 24 << 20, 12 << 20
CORE, X, Y = 1, 2, 4


beta_scale = 0.1
smooth_rate = 0.1


def swap(value, core0, core1):
    return lax.ppermute(
        value, "fsdp", [(i, i ^ (core1 if i & CORE else core0)) for i in range(8)]
    )


SMEM, VMEM, ANY = (
    pl.BlockSpec(memory_space=pltpu.SMEM),
    pl.BlockSpec(memory_space=pltpu.VMEM),
    pl.BlockSpec(memory_space=pl.ANY),
)


def places():
    me, plane = lax.axis_index("fsdp"), lax.axis_index("tp") & 1
    core, x_at, y_at = me & 1, (me >> 1) & 1, (me >> 2) & 1
    on_gate = core == 0
    far = me ^ jnp.where(on_gate, X, Y)
    straight = jnp.where(on_gate, x_at, y_at) == plane
    return [me, me ^ CORE, far, far ^ CORE], [straight, straight, ~straight, ~straight]


def find_slots(slot_at, col_slots, block_row, count, at_row):
    for r in range(count):
        for column in range(2 * col_slots.shape[1]):
            slot_at[at_row + r, column] = -1
        for slot in range(col_slots.shape[1]):
            slot_at[at_row + r, col_slots[block_row + r, slot]] = slot


def fill_dense(dense, weights, slot_at, at_row, column):
    for r in range(weights.shape[0] // BLK):
        for h in range(dense.shape[1] // BLK):
            slot = slot_at[at_row + r, column + h]
            at = pl.multiple_of(jnp.maximum(slot, 0) * BLK, BLK)
            block = weights[r * BLK : (r + 1) * BLK, pl.ds(at, BLK)]
            rows = slice((at_row + r) * BLK, (at_row + r + 1) * BLK)
            dense[rows, h * BLK : (h + 1) * BLK] = jnp.where(slot >= 0, block, jnp.zeros_like(block))


def early_kernel(
    col_slots, own, beside, direct, passed, mine, low, high, first,
    total, later, panel, weights, dense, slot_at, sems,
):
    depth, split = mine.shape[0], low.shape[1]
    rows = depth // BLK

    @pl.when(pl.program_id(0) == 0)
    def _():
        copies = [
            pltpu.make_async_copy(mine, weights.at[0], sems.at[0]),
            pltpu.make_async_copy(low, weights.at[1, :, :split], sems.at[1]),
            pltpu.make_async_copy(high, weights.at[1, :, split:], sems.at[2]),
            pltpu.make_async_copy(first, weights.at[2], sems.at[3]),
        ]
        for copy in copies:
            copy.start()
        count = own.shape[0]
        chunks, straight = places()
        for s in range(4):
            wide = pl.ds(pl.multiple_of(chunks[s] * depth, depth), depth)
            near = pl.ds(pl.multiple_of((chunks[s] & 1) * depth, depth), depth)
            groups = [
                own[:, wide],
                beside[:, wide],
                jnp.where(straight[s], direct[:, near], passed[:, near]),
            ]
            for group, start in zip(groups, (0, count, 2 * count)):
                at = slice(start, start + group.shape[0])
                if s < 3:
                    panel[at, s * depth : (s + 1) * depth] = group
                else:
                    later[at, :] = group
        for s in range(3):
            find_slots(slot_at, col_slots, chunks[s] * rows, rows, s * rows)
        for copy in copies:
            copy.wait()

    column = dense.shape[1] // BLK * pl.program_id(0)
    for s in range(3):
        fill_dense(dense, weights.at[s], slot_at, s * rows, column)
    total[...] = jnp.dot(panel[...], dense[...], preferred_element_type=jnp.float32)


def early_sums(col_slots, tokens, weights):
    count, (depth, width) = 4 * tokens[0].shape[0], weights[0].shape
    columns = 2 * col_slots.shape[1]
    step = 3 * 2 * BLK if columns % 6 == 0 else 2 * BLK
    return pl.pallas_call(
        early_kernel,
        grid=(columns * BLK // step,),
        out_shape=(
            jax.ShapeDtypeStruct((count, columns * BLK), jnp.float32),
            jax.ShapeDtypeStruct((count, depth), jnp.bfloat16),
        ),
        in_specs=[SMEM] + [VMEM] * 4 + [ANY] * 4,
        out_specs=(pl.BlockSpec((count, step), lambda n: (0, n)), VMEM),
        scratch_shapes=[
            pltpu.VMEM((count, 3 * depth), jnp.bfloat16),
            pltpu.VMEM((3, depth, width), jnp.bfloat16),
            pltpu.VMEM((3 * depth, step), jnp.bfloat16),
            pltpu.SMEM((3 * depth // BLK, columns), jnp.int32),
            pltpu.SemaphoreType.DMA((4,)),
        ],
        compiler_params=pltpu.CompilerParams(vmem_limit_bytes=EARLY_VMEM),
        cost_estimate=pl.CostEstimate(
            flops=2 * count * 3 * depth * columns * BLK,
            bytes_accessed=3 * depth * width * 2 + count * columns * BLK * 4,
            transcendentals=0,
        ),
    )(col_slots, *tokens, *weights)


def late_kernel(first_pair, col_slots, panel, early, *refs):
    parts, (mine, beside, near, weights, dense, slot_at, sems) = refs[:-7], refs[-7:]
    depth = weights.shape[0]
    rows = depth // BLK

    @pl.when(pl.program_id(0) == 0)
    def _():
        copies, start = [], 0
        for i, part in enumerate(parts):
            stop = start + part.shape[1]
            copies.append(pltpu.make_async_copy(part, weights.at[:, start:stop], sems.at[i]))
            start = stop
        for copy in copies:
            copy.start()
        find_slots(slot_at, col_slots, places()[0][3] * rows, rows, 0)
        for copy in copies:
            copy.wait()

    fill_dense(dense, weights, slot_at, 0, 2 * (first_pair + pl.program_id(0)))
    total = early[...] + jnp.dot(panel[...], dense[...], preferred_element_type=jnp.float32)
    count = mine.shape[0]
    mine[...] = total[:count]
    beside[...] = total[count : 2 * count]
    near[...] = total[2 * count :]


def late_sums(first_pair, pairs, col_slots, panel, early, parts):
    count, depth = panel.shape
    width = sum(part.shape[1] for part in parts)
    out_rows = (count // 4, count // 4, count // 2)
    return pl.pallas_call(
        functools.partial(late_kernel, first_pair),
        grid=(pairs,),
        out_shape=[
            jax.ShapeDtypeStruct((rows, pairs * 2 * BLK), jnp.float32) for rows in out_rows
        ],
        in_specs=[SMEM, VMEM, pl.BlockSpec((count, 2 * BLK), lambda n: (0, first_pair + n))]
        + [ANY] * len(parts),
        out_specs=[pl.BlockSpec((rows, 2 * BLK), lambda n: (0, n)) for rows in out_rows],
        scratch_shapes=[
            pltpu.VMEM((depth, width), jnp.bfloat16),
            pltpu.VMEM((depth, 2 * BLK), jnp.bfloat16),
            pltpu.SMEM((depth // BLK, 2 * col_slots.shape[1]), jnp.int32),
            pltpu.SemaphoreType.DMA((len(parts),)),
        ],
        compiler_params=pltpu.CompilerParams(vmem_limit_bytes=LATE_VMEM),
        cost_estimate=pl.CostEstimate(
            flops=2 * count * depth * pairs * 2 * BLK,
            bytes_accessed=depth * width * 2 + 2 * count * pairs * 2 * BLK * 4,
            transcendentals=0,
        ),
    )(col_slots, panel, early, *parts)


def pair_losses(token_terms, seq_lengths, pair_index, noise_flags):
    lengths = seq_lengths[0]
    seq_ends = jnp.cumsum(lengths)
    seq_starts = seq_ends - lengths
    positions = jnp.arange(token_terms.shape[0], dtype=jnp.int32)
    member = (positions[None, :] >= seq_starts[:, None]) & (positions[None, :] < seq_ends[:, None])
    share = jnp.sum(jnp.where(member, token_terms[None, :], jnp.float32(0.0)), axis=1)
    n_fsdp, n_tp = lax.axis_size("fsdp"), lax.axis_size("tp")
    spread = jnp.broadcast_to(share, (n_fsdp * n_tp, share.shape[0]))
    shares = lax.all_to_all(spread, ("fsdp", "tp"), 0, 0, tiled=True)
    ratios = jnp.sum(shares.reshape(n_fsdp, n_tp, share.shape[0]), axis=1).reshape(-1)
    seq_ids = jnp.arange(ratios.shape[0], dtype=jnp.int32)
    picked = jnp.sum(
        jnp.where(pair_index[:, :, None] == seq_ids, ratios, jnp.float32(0.0)), axis=2
    )
    sign_flip = 1.0 - 2.0 * noise_flags.astype(jnp.float32)
    margin = beta_scale * sign_flip * (picked[:, 0] - picked[:, 1])
    return -(1.0 - smooth_rate) * jax.nn.log_sigmoid(margin) - smooth_rate * jax.nn.log_sigmoid(
        -margin
    )


def gathered_parts(tokens, gate_packed, up_packed, col_slots):
    slot_count, row_count = col_slots.shape[1], col_slots.shape[0]
    column_ids = jnp.arange(2 * slot_count, dtype=jnp.int32)
    place = (col_slots[:, :, None] == column_ids[None, None, :]).astype(jnp.bfloat16)

    def product(packed):
        whole = lax.all_gather(packed, "fsdp", axis=0, tiled=True)
        blocks = whole.reshape(row_count, BLK, slot_count, BLK)
        dense = jnp.einsum("rnjc,rjm->rnmc", blocks, place, preferred_element_type=jnp.bfloat16)
        dense = dense.reshape(row_count * BLK, 2 * slot_count * BLK)
        return jnp.dot(tokens, dense, preferred_element_type=jnp.float32)

    return [(product(gate_packed), product(up_packed))]


def exchanged_parts(tokens, gate_packed, up_packed, col_slots):
    me, plane = lax.axis_index("fsdp"), lax.axis_index("tp") & 1
    core, x_at, y_at = me & 1, (me >> 1) & 1, (me >> 2) & 1
    on_gate = core == 0
    slot_count = col_slots.shape[1]
    third = 2 * slot_count // 3
    quarter = tokens.shape[1] // 4

    for_gate = lax.dynamic_slice_in_dim(tokens, (2 * (1 - y_at) + plane) * quarter, quarter, 1)
    for_up = lax.dynamic_slice_in_dim(tokens, (2 * plane + 1 - x_at) * quarter, quarter, 1)
    same = swap(jnp.where(on_gate, for_gate, for_up), Y, X)
    cross = swap(jnp.where(on_gate, for_up, for_gate), X | CORE, Y | CORE)
    gate_after, up_after, same, cross = lax.optimization_barrier(
        (gate_packed, up_packed, same, cross)
    )
    direct = jnp.concatenate([same, cross])
    passed = lax.ppermute(direct, "tp", [(i, i ^ 1) for i in range(lax.axis_size("tp"))])
    beside = swap(tokens, CORE, CORE)

    split = third * BLK
    low = swap(jnp.where(on_gate, up_packed[:, :split], gate_packed[:, :split]), CORE, CORE)
    high = swap(jnp.where(on_gate, up_packed[:, split:], gate_packed[:, split:]), CORE, CORE)
    mine = jnp.where(on_gate, gate_after, up_after)
    first = swap(mine, X, Y)
    far_low, far_high = swap(low, X, Y), swap(high, X, Y)

    early, panel = early_sums(col_slots, (tokens, beside, direct, passed), (mine, low, high, first))
    parts = []
    for n in range(3):
        sources = (far_low,) if n == 0 else (far_low, far_high)
        own, other, near = late_sums(
            n * third // 2, third // 2, col_slots, panel, early, sources
        )
        count = own.shape[0]
        near = near.astype(jnp.float16)
        own = own + swap(near[:count], Y, X).astype(jnp.float32)
        other = swap(other, CORE, CORE) + swap(near[count:], Y | CORE, X | CORE).astype(jnp.float32)
        parts.append((jnp.where(on_gate, own, other), jnp.where(on_gate, other, own)))
    return parts


def shards(
    tokens,
    gate_packed,
    up_packed,
    col_slots,
    readout,
    base_logp,
    ref_logp,
    seq_lengths,
    pair_index,
    noise_flags,
):
    whole = gate_packed.shape[0] % BLK == 0 and col_slots.shape[1] % 3 == 0
    by_core = lax.axis_size("fsdp") == 8 and lax.axis_size("tp") % 2 == 0 and whole
    sums = exchanged_parts if by_core else gathered_parts
    hiddens, contrib, done = [], 0.0, 0
    for gate_sum, up_sum in sums(tokens, gate_packed, up_packed, col_slots):
        hidden = (jax.nn.silu(gate_sum) * up_sum).astype(jnp.bfloat16)
        columns = slice(done, done + hidden.shape[1])
        contrib += jnp.dot(hidden, readout[columns], preferred_element_type=jnp.float32)
        hiddens.append(hidden)
        done = columns.stop
    hidden = jnp.concatenate(hiddens, axis=1)
    local_term = jnp.where(lax.axis_index("tp") == 0, base_logp - ref_logp, jnp.float32(0.0))
    return hidden, pair_losses(local_term + contrib, seq_lengths, pair_index, noise_flags)


def solution(mesh):
    in_specs = (
        P("fsdp", None),
        P("fsdp", "tp"),
        P("fsdp", "tp"),
        P(None, "tp"),
        P("tp"),
        P("fsdp"),
        P("fsdp"),
        P("fsdp", None),
        P("fsdp", None),
        P("fsdp"),
    )
    out_specs = (P("fsdp", "tp"), P("fsdp"))
    return jax.shard_map(shards, mesh=mesh, in_specs=in_specs, out_specs=out_specs, check_vma=False)
```

```python
import functools

import jax
import jax.numpy as jnp
from jax import lax
from jax.experimental import pallas as pl
from jax.experimental.pallas import tpu as pltpu
from jax.sharding import PartitionSpec as P

BLK = 128
EARLY_VMEM, LATE_VMEM = 18 << 20, 12 << 20
CORE, X, Y = 1, 2, 4


beta_scale = 0.1
smooth_rate = 0.1


def swap(value, core0, core1):
    return lax.ppermute(
        value, "fsdp", [(i, i ^ (core1 if i & CORE else core0)) for i in range(8)]
    )


SMEM, VMEM, ANY = (
    pl.BlockSpec(memory_space=pltpu.SMEM),
    pl.BlockSpec(memory_space=pltpu.VMEM),
    pl.BlockSpec(memory_space=pl.ANY),
)


def places():
    me, plane = lax.axis_index("fsdp"), lax.axis_index("tp") & 1
    core, x_at, y_at = me & 1, (me >> 1) & 1, (me >> 2) & 1
    on_gate = core == 0
    far = me ^ jnp.where(on_gate, X, Y)
    straight = jnp.where(on_gate, x_at, y_at) == plane
    return [me, me ^ CORE, far, far ^ CORE], [straight, straight, ~straight, ~straight]


def find_slots(slot_at, col_slots, block_row, count, at_row):
    for r in range(count):
        for column in range(2 * col_slots.shape[1]):
            slot_at[at_row + r, column] = -1
        for slot in range(col_slots.shape[1]):
            slot_at[at_row + r, col_slots[block_row + r, slot]] = slot


def fill_dense(dense, weights, slot_at, at_row, column):
    for r in range(weights.shape[0] // BLK):
        for h in range(dense.shape[1] // BLK):
            slot = slot_at[at_row + r, column + h]
            at = pl.multiple_of(jnp.maximum(slot, 0) * BLK, BLK)
            block = weights[r * BLK : (r + 1) * BLK, pl.ds(at, BLK)]
            rows = slice((at_row + r) * BLK, (at_row + r + 1) * BLK)
            dense[rows, h * BLK : (h + 1) * BLK] = jnp.where(slot >= 0, block, jnp.zeros_like(block))


def early_kernel(
    col_slots, own, direct, passed, mine, low, high, first,
    total, later, panel, weights, dense, slot_at, sems,
):
    depth, split = mine.shape[0], low.shape[1]
    rows = depth // BLK

    @pl.when(pl.program_id(0) == 0)
    def _():
        sources = [
            (mine, weights.at[0]),
            (low, weights.at[1, :, :split]),
            (high, weights.at[1, :, split:]),
            (first, weights.at[2]),
        ]
        chunks, straight = places()
        count = own.shape[0]
        targets = [panel.at[:, s * depth : (s + 1) * depth] for s in range(3)] + [later]
        for s in range(4):
            at = pl.multiple_of((s // 2 * 2 + (chunks[s] & 1)) * depth, depth)
            sources.append((own.at[:, pl.ds(at, depth)], targets[s].at[:count]))
        copies = [pltpu.make_async_copy(a, b, sems.at[n]) for n, (a, b) in enumerate(sources)]
        for copy in copies:
            copy.start()
        for s in range(4):
            near = pl.ds(pl.multiple_of((chunks[s] & 1) * depth, depth), depth)
            target, sem = targets[s].at[count:], sems.at[len(copies)]

            @pl.when(straight[s])
            def _():
                pltpu.make_async_copy(direct.at[:, near], target, sem).start()

            @pl.when(~straight[s])
            def _():
                pltpu.make_async_copy(passed.at[:, near], target, sem).start()

            copies.append(pltpu.make_async_copy(direct.at[:, near], target, sem))
        for s in range(3):
            find_slots(slot_at, col_slots, chunks[s] * rows, rows, s * rows)
        for copy in copies:
            copy.wait()

    column = dense.shape[1] // BLK * pl.program_id(0)
    for s in range(3):
        fill_dense(dense, weights.at[s], slot_at, s * rows, column)
    total[...] = jnp.dot(panel[...], dense[...], preferred_element_type=jnp.float32)


def early_sums(col_slots, tokens, weights):
    count, (depth, width) = 2 * tokens[0].shape[0], weights[0].shape
    columns = 2 * col_slots.shape[1]
    step = 3 * 2 * BLK if columns % 6 == 0 else 2 * BLK
    return pl.pallas_call(
        early_kernel,
        grid=(columns * BLK // step,),
        out_shape=(
            jax.ShapeDtypeStruct((count, columns * BLK), jnp.float32),
            jax.ShapeDtypeStruct((count, depth), jnp.bfloat16),
        ),
        in_specs=[SMEM] + [ANY] * 7,
        out_specs=(pl.BlockSpec((count, step), lambda n: (0, n)), VMEM),
        scratch_shapes=[
            pltpu.VMEM((count, 3 * depth), jnp.bfloat16),
            pltpu.VMEM((3, depth, width), jnp.bfloat16),
            pltpu.VMEM((3 * depth, step), jnp.bfloat16),
            pltpu.SMEM((3 * depth // BLK, columns), jnp.int32),
            pltpu.SemaphoreType.DMA((12,)),
        ],
        compiler_params=pltpu.CompilerParams(vmem_limit_bytes=EARLY_VMEM),
        cost_estimate=pl.CostEstimate(
            flops=2 * count * 3 * depth * columns * BLK,
            bytes_accessed=3 * depth * width * 2 + count * columns * BLK * 4,
            transcendentals=0,
        ),
    )(col_slots, *tokens, *weights)


def late_kernel(first_pair, col_slots, panel, early, *refs):
    parts, (mine, beside, near, weights, dense, slot_at, sems) = refs[:-7], refs[-7:]
    depth = weights.shape[0]
    rows = depth // BLK

    @pl.when(pl.program_id(0) == 0)
    def _():
        copies, start = [], 0
        for i, part in enumerate(parts):
            stop = start + part.shape[1]
            copies.append(pltpu.make_async_copy(part, weights.at[:, start:stop], sems.at[i]))
            start = stop
        for copy in copies:
            copy.start()
        find_slots(slot_at, col_slots, places()[0][3] * rows, rows, 0)
        for copy in copies:
            copy.wait()

    fill_dense(dense, weights, slot_at, 0, 2 * (first_pair + pl.program_id(0)))
    total = early[...] + jnp.dot(panel[...], dense[...], preferred_element_type=jnp.float32)
    count = mine.shape[0]
    mine[...] = total[:count]
    beside[...] = total[count : 2 * count]
    near[...] = total[2 * count :]


def late_sums(first_pair, pairs, col_slots, panel, early, parts):
    count, depth = panel.shape
    width = sum(part.shape[1] for part in parts)
    out_rows = (count // 4, count // 4, count // 2)
    return pl.pallas_call(
        functools.partial(late_kernel, first_pair),
        grid=(pairs,),
        out_shape=[
            jax.ShapeDtypeStruct((rows, pairs * 2 * BLK), jnp.float32) for rows in out_rows
        ],
        in_specs=[SMEM, VMEM, pl.BlockSpec((count, 2 * BLK), lambda n: (0, first_pair + n))]
        + [ANY] * len(parts),
        out_specs=[pl.BlockSpec((rows, 2 * BLK), lambda n: (0, n)) for rows in out_rows],
        scratch_shapes=[
            pltpu.VMEM((depth, width), jnp.bfloat16),
            pltpu.VMEM((depth, 2 * BLK), jnp.bfloat16),
            pltpu.SMEM((depth // BLK, 2 * col_slots.shape[1]), jnp.int32),
            pltpu.SemaphoreType.DMA((len(parts),)),
        ],
        compiler_params=pltpu.CompilerParams(vmem_limit_bytes=LATE_VMEM),
        cost_estimate=pl.CostEstimate(
            flops=2 * count * depth * pairs * 2 * BLK,
            bytes_accessed=depth * width * 2 + 2 * count * pairs * 2 * BLK * 4,
            transcendentals=0,
        ),
    )(col_slots, panel, early, *parts)


def pair_losses(token_terms, seq_lengths, pair_index, noise_flags):
    lengths = seq_lengths[0]
    seq_ends = jnp.cumsum(lengths)
    seq_starts = seq_ends - lengths
    positions = jnp.arange(token_terms.shape[0], dtype=jnp.int32)
    member = (positions[None, :] >= seq_starts[:, None]) & (positions[None, :] < seq_ends[:, None])
    share = jnp.sum(jnp.where(member, token_terms[None, :], jnp.float32(0.0)), axis=1)
    n_fsdp, n_tp = lax.axis_size("fsdp"), lax.axis_size("tp")
    spread = jnp.broadcast_to(share, (n_fsdp * n_tp, share.shape[0]))
    shares = lax.all_to_all(spread, ("fsdp", "tp"), 0, 0, tiled=True)
    ratios = jnp.sum(shares.reshape(n_fsdp, n_tp, share.shape[0]), axis=1).reshape(-1)
    seq_ids = jnp.arange(ratios.shape[0], dtype=jnp.int32)
    picked = jnp.sum(
        jnp.where(pair_index[:, :, None] == seq_ids, ratios, jnp.float32(0.0)), axis=2
    )
    sign_flip = 1.0 - 2.0 * noise_flags.astype(jnp.float32)
    margin = beta_scale * sign_flip * (picked[:, 0] - picked[:, 1])
    return -(1.0 - smooth_rate) * jax.nn.log_sigmoid(margin) - smooth_rate * jax.nn.log_sigmoid(
        -margin
    )


def gathered_parts(tokens, gate_packed, up_packed, col_slots):
    slot_count, row_count = col_slots.shape[1], col_slots.shape[0]
    column_ids = jnp.arange(2 * slot_count, dtype=jnp.int32)
    place = (col_slots[:, :, None] == column_ids[None, None, :]).astype(jnp.bfloat16)

    def product(packed):
        whole = lax.all_gather(packed, "fsdp", axis=0, tiled=True)
        blocks = whole.reshape(row_count, BLK, slot_count, BLK)
        dense = jnp.einsum("rnjc,rjm->rnmc", blocks, place, preferred_element_type=jnp.bfloat16)
        dense = dense.reshape(row_count * BLK, 2 * slot_count * BLK)
        return jnp.dot(tokens, dense, preferred_element_type=jnp.float32)

    return [(product(gate_packed), product(up_packed))]


def exchanged_parts(tokens, gate_packed, up_packed, col_slots):
    me, plane = lax.axis_index("fsdp"), lax.axis_index("tp") & 1
    core, x_at, y_at = me & 1, (me >> 1) & 1, (me >> 2) & 1
    on_gate = core == 0
    slot_count = col_slots.shape[1]
    third = 2 * slot_count // 3
    quarter = tokens.shape[1] // 4

    beside = swap(tokens, CORE, CORE)
    mine = jnp.where(on_gate, gate_packed, up_packed)
    first = swap(mine, X, Y)
    start = quarter * jnp.where(on_gate, 2 * (1 - y_at) + plane, 2 * plane + 1 - x_at)
    quarters = [lax.dynamic_slice_in_dim(rows, start, quarter, 1) for rows in (tokens, beside)]
    direct = swap(jnp.concatenate(quarters), Y, X)
    tokens_after, beside, direct = lax.optimization_barrier((tokens, beside, direct))
    passed = lax.ppermute(direct, "tp", [(i, i ^ 1) for i in range(lax.axis_size("tp"))])
    split = third * BLK
    low = swap(jnp.where(on_gate, up_packed[:, :split], gate_packed[:, :split]), CORE, CORE)
    high = swap(jnp.where(on_gate, up_packed[:, split:], gate_packed[:, split:]), CORE, CORE)
    far_low = swap(low, X, Y)
    high, passed = lax.optimization_barrier((high, passed))
    far_high = swap(high, X, Y)
    chip = me >> 1
    far_chip = chip ^ jnp.where(on_gate, 1, 2)
    both = jnp.concatenate([tokens_after, beside])
    own = jnp.concatenate(
        [lax.dynamic_slice_in_dim(both, at * quarter, quarter, 1) for at in (chip, far_chip)], axis=1
    )

    early, panel = early_sums(col_slots, (own, direct, passed), (mine, low, high, first))
    parts = []
    for n in range(3):
        sources = (far_low,) if n == 0 else (far_low, far_high)
        own, other, near = late_sums(
            n * third // 2, third // 2, col_slots, panel, early, sources
        )
        count = own.shape[0]
        near = near.astype(jnp.float16)
        own = own + swap(near[:count], Y, X).astype(jnp.float32)
        other = swap(other, CORE, CORE) + swap(near[count:], Y | CORE, X | CORE).astype(jnp.float32)
        parts.append((jnp.where(on_gate, own, other), jnp.where(on_gate, other, own)))
    return parts


def shards(
    tokens,
    gate_packed,
    up_packed,
    col_slots,
    readout,
    base_logp,
    ref_logp,
    seq_lengths,
    pair_index,
    noise_flags,
):
    whole = gate_packed.shape[0] % BLK == 0 and col_slots.shape[1] % 3 == 0
    by_core = lax.axis_size("fsdp") == 8 and lax.axis_size("tp") % 2 == 0 and whole
    sums = exchanged_parts if by_core else gathered_parts
    hiddens, contrib, done = [], 0.0, 0
    for gate_sum, up_sum in sums(tokens, gate_packed, up_packed, col_slots):
        hidden = (jax.nn.silu(gate_sum) * up_sum).astype(jnp.bfloat16)
        columns = slice(done, done + hidden.shape[1])
        contrib += jnp.dot(hidden, readout[columns], preferred_element_type=jnp.float32)
        hiddens.append(hidden)
        done = columns.stop
    hidden = jnp.concatenate(hiddens, axis=1)
    local_term = jnp.where(lax.axis_index("tp") == 0, base_logp - ref_logp, jnp.float32(0.0))
    return hidden, pair_losses(local_term + contrib, seq_lengths, pair_index, noise_flags)


def solution(mesh):
    in_specs = (
        P("fsdp", None),
        P("fsdp", "tp"),
        P("fsdp", "tp"),
        P(None, "tp"),
        P("tp"),
        P("fsdp"),
        P("fsdp"),
        P("fsdp", None),
        P("fsdp", None),
        P("fsdp"),
    )
    out_specs = (P("fsdp", "tp"), P("fsdp"))
    return jax.shard_map(shards, mesh=mesh, in_specs=in_specs, out_specs=out_specs, check_vma=False)
```

```python
import functools

import jax
import jax.numpy as jnp
from jax import lax
from jax.experimental import pallas as pl
from jax.experimental.pallas import tpu as pltpu
from jax.sharding import PartitionSpec as P

BLK = 128
EARLY_VMEM, LATE_VMEM = 18 << 20, 12 << 20
HEAD = 3 * BLK // 2
CORE, X, Y = 1, 2, 4


beta_scale = 0.1
smooth_rate = 0.1


def swap(value, core0, core1):
    return lax.ppermute(
        value, "fsdp", [(i, i ^ (core1 if i & CORE else core0)) for i in range(8)]
    )


SMEM, VMEM, ANY = (
    pl.BlockSpec(memory_space=pltpu.SMEM),
    pl.BlockSpec(memory_space=pltpu.VMEM),
    pl.BlockSpec(memory_space=pl.ANY),
)


def places():
    me, plane = lax.axis_index("fsdp"), lax.axis_index("tp") & 1
    core, x_at, y_at = me & 1, (me >> 1) & 1, (me >> 2) & 1
    on_gate = core == 0
    far = me ^ jnp.where(on_gate, X, Y)
    straight = jnp.where(on_gate, x_at, y_at) == plane
    return [me, me ^ CORE, far, far ^ CORE], [straight, straight, ~straight, ~straight]


def find_slots(slot_at, col_slots, block_row, count, at_row):
    for r in range(count):
        for column in range(2 * col_slots.shape[1]):
            slot_at[at_row + r, column] = -1
        for slot in range(col_slots.shape[1]):
            slot_at[at_row + r, col_slots[block_row + r, slot]] = slot


def fill_dense(dense, weights, slot_at, at_row, column):
    for r in range(weights.shape[0] // BLK):
        for h in range(dense.shape[1] // BLK):
            slot = slot_at[at_row + r, column + h]
            at = pl.multiple_of(jnp.maximum(slot, 0) * BLK, BLK)
            block = weights[r * BLK : (r + 1) * BLK, pl.ds(at, BLK)]
            rows = slice((at_row + r) * BLK, (at_row + r + 1) * BLK)
            dense[rows, h * BLK : (h + 1) * BLK] = jnp.where(slot >= 0, block, jnp.zeros_like(block))


def early_kernel(
    col_slots, own, direct, passed, mine1, mine2, low, high, first1, first2,
    total, later, panel, weights, dense, slot_at, sems,
):
    (depth, split), head = low.shape, mine1.shape[0]
    rows = depth // BLK

    @pl.when(pl.program_id(0) == 0)
    def _():
        sources = [
            (mine1, weights.at[0, :head]),
            (mine2, weights.at[0, head:]),
            (low, weights.at[1, :, :split]),
            (high, weights.at[1, :, split:]),
            (first1, weights.at[2, :head]),
            (first2, weights.at[2, head:]),
        ]
        chunks, straight = places()
        count = own.shape[0]
        targets = [panel.at[:, s * depth : (s + 1) * depth] for s in range(3)] + [later]
        for s in range(4):
            at = pl.multiple_of((s // 2 * 2 + (chunks[s] & 1)) * depth, depth)
            sources.append((own.at[:, pl.ds(at, depth)], targets[s].at[:count]))
        copies = [pltpu.make_async_copy(a, b, sems.at[n]) for n, (a, b) in enumerate(sources)]
        for copy in copies:
            copy.start()
        for s in range(4):
            near = pl.ds(pl.multiple_of((chunks[s] & 1) * depth, depth), depth)
            target, sem = targets[s].at[count:], sems.at[len(copies)]

            @pl.when(straight[s])
            def _():
                pltpu.make_async_copy(direct.at[:, near], target, sem).start()

            @pl.when(~straight[s])
            def _():
                pltpu.make_async_copy(passed.at[:, near], target, sem).start()

            copies.append(pltpu.make_async_copy(direct.at[:, near], target, sem))
        for s in range(3):
            find_slots(slot_at, col_slots, chunks[s] * rows, rows, s * rows)
        for copy in copies:
            copy.wait()

    column = dense.shape[1] // BLK * pl.program_id(0)
    for s in range(3):
        fill_dense(dense, weights.at[s], slot_at, s * rows, column)
    total[...] = jnp.dot(panel[...], dense[...], preferred_element_type=jnp.float32)


def early_sums(col_slots, tokens, weights):
    count, depth, width = 2 * tokens[0].shape[0], weights[2].shape[0], weights[0].shape[1]
    columns = 2 * col_slots.shape[1]
    step = 3 * 2 * BLK if columns % 6 == 0 else 2 * BLK
    return pl.pallas_call(
        early_kernel,
        grid=(columns * BLK // step,),
        out_shape=(
            jax.ShapeDtypeStruct((count, columns * BLK), jnp.float32),
            jax.ShapeDtypeStruct((count, depth), jnp.bfloat16),
        ),
        in_specs=[SMEM] + [ANY] * 9,
        out_specs=(pl.BlockSpec((count, step), lambda n: (0, n)), VMEM),
        scratch_shapes=[
            pltpu.VMEM((count, 3 * depth), jnp.bfloat16),
            pltpu.VMEM((3, depth, width), jnp.bfloat16),
            pltpu.VMEM((3 * depth, step), jnp.bfloat16),
            pltpu.SMEM((3 * depth // BLK, columns), jnp.int32),
            pltpu.SemaphoreType.DMA((14,)),
        ],
        compiler_params=pltpu.CompilerParams(vmem_limit_bytes=EARLY_VMEM),
        cost_estimate=pl.CostEstimate(
            flops=2 * count * 3 * depth * columns * BLK,
            bytes_accessed=3 * depth * width * 2 + count * columns * BLK * 4,
            transcendentals=0,
        ),
    )(col_slots, *tokens, *weights)


def late_kernel(first_pair, col_slots, panel, early, *refs):
    parts, (mine, beside, near, weights, dense, slot_at, sems) = refs[:-7], refs[-7:]
    depth = weights.shape[0]
    rows = depth // BLK

    @pl.when(pl.program_id(0) == 0)
    def _():
        copies, start = [], 0
        for i, part in enumerate(parts):
            stop = start + part.shape[1]
            copies.append(pltpu.make_async_copy(part, weights.at[:, start:stop], sems.at[i]))
            start = stop
        for copy in copies:
            copy.start()
        find_slots(slot_at, col_slots, places()[0][3] * rows, rows, 0)
        for copy in copies:
            copy.wait()

    fill_dense(dense, weights, slot_at, 0, 2 * (first_pair + pl.program_id(0)))
    total = early[...] + jnp.dot(panel[...], dense[...], preferred_element_type=jnp.float32)
    count = mine.shape[0]
    mine[...] = total[:count]
    beside[...] = total[count : 2 * count]
    near[...] = total[2 * count :]


def late_sums(first_pair, pairs, col_slots, panel, early, parts):
    count, depth = panel.shape
    width = sum(part.shape[1] for part in parts)
    out_rows = (count // 4, count // 4, count // 2)
    return pl.pallas_call(
        functools.partial(late_kernel, first_pair),
        grid=(pairs,),
        out_shape=[
            jax.ShapeDtypeStruct((rows, pairs * 2 * BLK), jnp.float32) for rows in out_rows
        ],
        in_specs=[SMEM, VMEM, pl.BlockSpec((count, 2 * BLK), lambda n: (0, first_pair + n))]
        + [ANY] * len(parts),
        out_specs=[pl.BlockSpec((rows, 2 * BLK), lambda n: (0, n)) for rows in out_rows],
        scratch_shapes=[
            pltpu.VMEM((depth, width), jnp.bfloat16),
            pltpu.VMEM((depth, 2 * BLK), jnp.bfloat16),
            pltpu.SMEM((depth // BLK, 2 * col_slots.shape[1]), jnp.int32),
            pltpu.SemaphoreType.DMA((len(parts),)),
        ],
        compiler_params=pltpu.CompilerParams(vmem_limit_bytes=LATE_VMEM),
        cost_estimate=pl.CostEstimate(
            flops=2 * count * depth * pairs * 2 * BLK,
            bytes_accessed=depth * width * 2 + 2 * count * pairs * 2 * BLK * 4,
            transcendentals=0,
        ),
    )(col_slots, panel, early, *parts)


def pair_losses(token_terms, seq_lengths, pair_index, noise_flags):
    lengths = seq_lengths[0]
    seq_ends = jnp.cumsum(lengths)
    seq_starts = seq_ends - lengths
    positions = jnp.arange(token_terms.shape[0], dtype=jnp.int32)
    member = (positions[None, :] >= seq_starts[:, None]) & (positions[None, :] < seq_ends[:, None])
    share = jnp.sum(jnp.where(member, token_terms[None, :], jnp.float32(0.0)), axis=1)
    n_fsdp, n_tp = lax.axis_size("fsdp"), lax.axis_size("tp")
    spread = jnp.broadcast_to(share, (n_fsdp * n_tp, share.shape[0]))
    shares = lax.all_to_all(spread, ("fsdp", "tp"), 0, 0, tiled=True)
    ratios = jnp.sum(shares.reshape(n_fsdp, n_tp, share.shape[0]), axis=1).reshape(-1)
    seq_ids = jnp.arange(ratios.shape[0], dtype=jnp.int32)
    picked = jnp.sum(
        jnp.where(pair_index[:, :, None] == seq_ids, ratios, jnp.float32(0.0)), axis=2
    )
    sign_flip = 1.0 - 2.0 * noise_flags.astype(jnp.float32)
    margin = beta_scale * sign_flip * (picked[:, 0] - picked[:, 1])
    return -(1.0 - smooth_rate) * jax.nn.log_sigmoid(margin) - smooth_rate * jax.nn.log_sigmoid(
        -margin
    )


def gathered_parts(tokens, gate_packed, up_packed, col_slots):
    slot_count, row_count = col_slots.shape[1], col_slots.shape[0]
    column_ids = jnp.arange(2 * slot_count, dtype=jnp.int32)
    place = (col_slots[:, :, None] == column_ids[None, None, :]).astype(jnp.bfloat16)

    def product(packed):
        whole = lax.all_gather(packed, "fsdp", axis=0, tiled=True)
        blocks = whole.reshape(row_count, BLK, slot_count, BLK)
        dense = jnp.einsum("rnjc,rjm->rnmc", blocks, place, preferred_element_type=jnp.bfloat16)
        dense = dense.reshape(row_count * BLK, 2 * slot_count * BLK)
        return jnp.dot(tokens, dense, preferred_element_type=jnp.float32)

    return [(product(gate_packed), product(up_packed))]


def exchanged_parts(tokens, gate_packed, up_packed, col_slots):
    me, plane = lax.axis_index("fsdp"), lax.axis_index("tp") & 1
    core, x_at, y_at = me & 1, (me >> 1) & 1, (me >> 2) & 1
    on_gate = core == 0
    slot_count = col_slots.shape[1]
    third = 2 * slot_count // 3
    quarter = tokens.shape[1] // 4

    beside = swap(tokens, CORE, CORE)
    mine = [
        jnp.where(on_gate, gate_packed[:HEAD], up_packed[:HEAD]),
        jnp.where(on_gate, gate_packed[HEAD:], up_packed[HEAD:]),
    ]
    first = [swap(mine[0], X, Y)]
    gate_after, up_after, mine[1], first[0] = lax.optimization_barrier(
        (gate_packed, up_packed, mine[1], first[0])
    )
    first.append(swap(mine[1], X, Y))
    start = quarter * jnp.where(on_gate, 2 * (1 - y_at) + plane, 2 * plane + 1 - x_at)
    quarters = [lax.dynamic_slice_in_dim(rows, start, quarter, 1) for rows in (tokens, beside)]
    direct = swap(jnp.concatenate(quarters), Y, X)
    tokens_after, beside, direct = lax.optimization_barrier((tokens, beside, direct))
    passed = lax.ppermute(direct, "tp", [(i, i ^ 1) for i in range(lax.axis_size("tp"))])
    split = third * BLK
    low = swap(jnp.where(on_gate, up_packed[:, :split], gate_packed[:, :split]), CORE, CORE)
    high = swap(jnp.where(on_gate, up_after[:, split:], gate_after[:, split:]), CORE, CORE)
    far_low = swap(low, X, Y)
    high, passed = lax.optimization_barrier((high, passed))
    far_high = swap(high, X, Y)
    chip = me >> 1
    far_chip = chip ^ jnp.where(on_gate, 1, 2)
    both = jnp.concatenate([tokens_after, beside])
    own = jnp.concatenate(
        [lax.dynamic_slice_in_dim(both, at * quarter, quarter, 1) for at in (chip, far_chip)], axis=1
    )

    early, panel = early_sums(col_slots, (own, direct, passed), (*mine, low, high, *first))
    parts = []
    for n in range(3):
        sources = (far_low,) if n == 0 else (far_low, far_high)
        own, other, near = late_sums(
            n * third // 2, third // 2, col_slots, panel, early, sources
        )
        count = own.shape[0]
        near = near.astype(jnp.float16)
        own = own + swap(near[:count], Y, X).astype(jnp.float32)
        other = swap(other, CORE, CORE) + swap(near[count:], Y | CORE, X | CORE).astype(jnp.float32)
        parts.append((jnp.where(on_gate, own, other), jnp.where(on_gate, other, own)))
    return parts


def shards(
    tokens,
    gate_packed,
    up_packed,
    col_slots,
    readout,
    base_logp,
    ref_logp,
    seq_lengths,
    pair_index,
    noise_flags,
):
    whole = gate_packed.shape[0] % BLK == 0 and col_slots.shape[1] % 3 == 0
    by_core = lax.axis_size("fsdp") == 8 and lax.axis_size("tp") % 2 == 0 and whole
    sums = exchanged_parts if by_core else gathered_parts
    hiddens, contrib, done = [], 0.0, 0
    for gate_sum, up_sum in sums(tokens, gate_packed, up_packed, col_slots):
        hidden = (jax.nn.silu(gate_sum) * up_sum).astype(jnp.bfloat16)
        columns = slice(done, done + hidden.shape[1])
        contrib += jnp.dot(hidden, readout[columns], preferred_element_type=jnp.float32)
        hiddens.append(hidden)
        done = columns.stop
    hidden = jnp.concatenate(hiddens, axis=1)
    local_term = jnp.where(lax.axis_index("tp") == 0, base_logp - ref_logp, jnp.float32(0.0))
    return hidden, pair_losses(local_term + contrib, seq_lengths, pair_index, noise_flags)


def solution(mesh):
    in_specs = (
        P("fsdp", None),
        P("fsdp", "tp"),
        P("fsdp", "tp"),
        P(None, "tp"),
        P("tp"),
        P("fsdp"),
        P("fsdp"),
        P("fsdp", None),
        P("fsdp", None),
        P("fsdp"),
    )
    out_specs = (P("fsdp", "tp"), P("fsdp"))
    return jax.shard_map(shards, mesh=mesh, in_specs=in_specs, out_specs=out_specs, check_vma=False)
```

```python
import functools

import jax
import jax.numpy as jnp
from jax import lax
from jax.experimental import pallas as pl
from jax.experimental.pallas import tpu as pltpu
from jax.sharding import PartitionSpec as P

BLK = 128
EARLY_VMEM, LATE_VMEM = 18 << 20, 12 << 20
HEAD = 3 * BLK // 2
CORE, X, Y = 1, 2, 4


beta_scale = 0.1
smooth_rate = 0.1


def swap(value, core0, core1):
    return lax.ppermute(
        value, "fsdp", [(i, i ^ (core1 if i & CORE else core0)) for i in range(8)]
    )


SMEM, VMEM, ANY = (
    pl.BlockSpec(memory_space=pltpu.SMEM),
    pl.BlockSpec(memory_space=pltpu.VMEM),
    pl.BlockSpec(memory_space=pl.ANY),
)


def places():
    me, plane = lax.axis_index("fsdp"), lax.axis_index("tp") & 1
    core, x_at, y_at = me & 1, (me >> 1) & 1, (me >> 2) & 1
    on_gate = core == 0
    far = me ^ jnp.where(on_gate, X, Y)
    straight = jnp.where(on_gate, x_at, y_at) == plane
    return [me, me ^ CORE, far, far ^ CORE], [straight, straight, ~straight, ~straight]


def find_slots(slot_at, col_slots, block_row, count, at_row):
    for r in range(count):
        for column in range(2 * col_slots.shape[1]):
            slot_at[at_row + r, column] = -1
        for slot in range(col_slots.shape[1]):
            slot_at[at_row + r, col_slots[block_row + r, slot]] = slot


def fill_dense(dense, weights, slot_at, at_row, column):
    for r in range(weights.shape[0] // BLK):
        for h in range(dense.shape[1] // BLK):
            slot = slot_at[at_row + r, column + h]
            at = pl.multiple_of(jnp.maximum(slot, 0) * BLK, BLK)
            block = weights[r * BLK : (r + 1) * BLK, pl.ds(at, BLK)]
            rows = slice((at_row + r) * BLK, (at_row + r + 1) * BLK)
            dense[rows, h * BLK : (h + 1) * BLK] = jnp.where(slot >= 0, block, jnp.zeros_like(block))


def early_kernel(
    col_slots, own, direct, passed, mine1, mine2, low, high, first1, first2,
    total, later, panel, weights, dense, slot_at, sems,
):
    (depth, split), head = low.shape, mine1.shape[0]
    rows = depth // BLK

    @pl.when(pl.program_id(0) == 0)
    def _():
        sources = [
            (mine1, weights.at[0, :head]),
            (mine2, weights.at[0, head:]),
            (low, weights.at[1, :, :split]),
            (high, weights.at[1, :, split:]),
            (first1, weights.at[2, :head]),
            (first2, weights.at[2, head:]),
        ]
        chunks, straight = places()
        count = own.shape[0]
        targets = [panel.at[:, s * depth : (s + 1) * depth] for s in range(3)] + [later]
        for s in range(4):
            at = pl.multiple_of((s // 2 * 2 + (chunks[s] & 1)) * depth, depth)
            sources.append((own.at[:, pl.ds(at, depth)], targets[s].at[:count]))
        copies = [pltpu.make_async_copy(a, b, sems.at[n]) for n, (a, b) in enumerate(sources)]
        for copy in copies:
            copy.start()
        for s in range(4):
            near = pl.ds(pl.multiple_of((chunks[s] & 1) * depth, depth), depth)
            target, sem = targets[s].at[count:], sems.at[len(copies)]

            @pl.when(straight[s])
            def _():
                pltpu.make_async_copy(direct.at[:, near], target, sem).start()

            @pl.when(~straight[s])
            def _():
                pltpu.make_async_copy(passed.at[:, near], target, sem).start()

            copies.append(pltpu.make_async_copy(direct.at[:, near], target, sem))
        for s in range(3):
            find_slots(slot_at, col_slots, chunks[s] * rows, rows, s * rows)
        for copy in copies:
            copy.wait()

    column = dense.shape[1] // BLK * pl.program_id(0)
    for s in range(3):
        fill_dense(dense, weights.at[s], slot_at, s * rows, column)
    total[...] = jnp.dot(panel[...], dense[...], preferred_element_type=jnp.float32)


def early_sums(col_slots, tokens, weights):
    count, depth, width = 2 * tokens[0].shape[0], weights[2].shape[0], weights[0].shape[1]
    columns = 2 * col_slots.shape[1]
    step = 3 * 2 * BLK if columns % 6 == 0 else 2 * BLK
    return pl.pallas_call(
        early_kernel,
        grid=(columns * BLK // step,),
        out_shape=(
            jax.ShapeDtypeStruct((count, columns * BLK), jnp.float32),
            jax.ShapeDtypeStruct((count, depth), jnp.bfloat16),
        ),
        in_specs=[SMEM] + [ANY] * 9,
        out_specs=(pl.BlockSpec((count, step), lambda n: (0, n)), VMEM),
        scratch_shapes=[
            pltpu.VMEM((count, 3 * depth), jnp.bfloat16),
            pltpu.VMEM((3, depth, width), jnp.bfloat16),
            pltpu.VMEM((3 * depth, step), jnp.bfloat16),
            pltpu.SMEM((3 * depth // BLK, columns), jnp.int32),
            pltpu.SemaphoreType.DMA((14,)),
        ],
        compiler_params=pltpu.CompilerParams(vmem_limit_bytes=EARLY_VMEM),
        cost_estimate=pl.CostEstimate(
            flops=2 * count * 3 * depth * columns * BLK,
            bytes_accessed=3 * depth * width * 2 + count * columns * BLK * 4,
            transcendentals=0,
        ),
    )(col_slots, *tokens, *weights)


def late_kernel(first_column, col_slots, panel, early, *refs):
    parts, (mine, beside, near, dense, slot_at) = refs[:-5], refs[-5:]
    rows, lasts = panel.shape[1] // BLK, [part.shape[1] // BLK for part in parts]

    @pl.when(pl.program_id(0) == 0)
    def _():
        find_slots(slot_at, col_slots, places()[0][3] * rows, rows, 0)

    column = first_column + dense.shape[1] // BLK * pl.program_id(0)
    for r in range(rows):
        at_rows = slice(r * BLK, (r + 1) * BLK)
        for h in range(dense.shape[1] // BLK):
            slot = slot_at[r, column + h]
            block, before = jnp.zeros((BLK, BLK), dense.dtype), 0
            for part, count in zip(parts, lasts):
                at = pl.multiple_of(jnp.clip(slot - before, 0, count - 1) * BLK, BLK)
                block = jnp.where(slot >= before, part[at_rows, pl.ds(at, BLK)], block)
                before += count
            dense[at_rows, h * BLK : (h + 1) * BLK] = block
    total = early[...] + jnp.dot(panel[...], dense[...], preferred_element_type=jnp.float32)
    count = mine.shape[0]
    mine[...] = total[:count]
    beside[...] = total[count : 2 * count]
    near[...] = total[2 * count :]


def late_sums(first_pair, pairs, col_slots, panel, early, parts):
    count, depth = panel.shape
    width = sum(part.shape[1] for part in parts)
    out_rows = (count // 4, count // 4, count // 2)
    step = pairs * BLK
    first = 2 * first_pair * BLK // step
    return pl.pallas_call(
        functools.partial(late_kernel, 2 * first_pair),
        grid=(pairs * 2 * BLK // step,),
        out_shape=[
            jax.ShapeDtypeStruct((rows, pairs * 2 * BLK), jnp.float32) for rows in out_rows
        ],
        in_specs=[SMEM, VMEM, pl.BlockSpec((count, step), lambda n: (0, first + n))]
        + [VMEM] * len(parts),
        out_specs=[pl.BlockSpec((rows, step), lambda n: (0, n)) for rows in out_rows],
        scratch_shapes=[
            pltpu.VMEM((depth, step), jnp.bfloat16),
            pltpu.SMEM((depth // BLK, 2 * col_slots.shape[1]), jnp.int32),
        ],
        compiler_params=pltpu.CompilerParams(vmem_limit_bytes=LATE_VMEM),
        cost_estimate=pl.CostEstimate(
            flops=2 * count * depth * pairs * 2 * BLK,
            bytes_accessed=depth * width * 2 + 2 * count * pairs * 2 * BLK * 4,
            transcendentals=0,
        ),
    )(col_slots, panel, early, *parts)


def pair_losses(token_terms, seq_lengths, pair_index, noise_flags):
    lengths = seq_lengths[0]
    seq_ends = jnp.cumsum(lengths)
    seq_starts = seq_ends - lengths
    positions = jnp.arange(token_terms.shape[0], dtype=jnp.int32)
    member = (positions[None, :] >= seq_starts[:, None]) & (positions[None, :] < seq_ends[:, None])
    share = jnp.sum(jnp.where(member, token_terms[None, :], jnp.float32(0.0)), axis=1)
    n_fsdp, n_tp = lax.axis_size("fsdp"), lax.axis_size("tp")
    spread = jnp.broadcast_to(share, (n_fsdp * n_tp, share.shape[0]))
    shares = lax.all_to_all(spread, ("fsdp", "tp"), 0, 0, tiled=True)
    ratios = jnp.sum(shares.reshape(n_fsdp, n_tp, share.shape[0]), axis=1).reshape(-1)
    seq_ids = jnp.arange(ratios.shape[0], dtype=jnp.int32)
    picked = jnp.sum(
        jnp.where(pair_index[:, :, None] == seq_ids, ratios, jnp.float32(0.0)), axis=2
    )
    sign_flip = 1.0 - 2.0 * noise_flags.astype(jnp.float32)
    margin = beta_scale * sign_flip * (picked[:, 0] - picked[:, 1])
    return -(1.0 - smooth_rate) * jax.nn.log_sigmoid(margin) - smooth_rate * jax.nn.log_sigmoid(
        -margin
    )


def gathered_parts(tokens, gate_packed, up_packed, col_slots):
    slot_count, row_count = col_slots.shape[1], col_slots.shape[0]
    column_ids = jnp.arange(2 * slot_count, dtype=jnp.int32)
    place = (col_slots[:, :, None] == column_ids[None, None, :]).astype(jnp.bfloat16)

    def product(packed):
        whole = lax.all_gather(packed, "fsdp", axis=0, tiled=True)
        blocks = whole.reshape(row_count, BLK, slot_count, BLK)
        dense = jnp.einsum("rnjc,rjm->rnmc", blocks, place, preferred_element_type=jnp.bfloat16)
        dense = dense.reshape(row_count * BLK, 2 * slot_count * BLK)
        return jnp.dot(tokens, dense, preferred_element_type=jnp.float32)

    return [(product(gate_packed), product(up_packed))]


def exchanged_parts(tokens, gate_packed, up_packed, col_slots):
    me, plane = lax.axis_index("fsdp"), lax.axis_index("tp") & 1
    core, x_at, y_at = me & 1, (me >> 1) & 1, (me >> 2) & 1
    on_gate = core == 0
    slot_count = col_slots.shape[1]
    third = 2 * slot_count // 3
    quarter = tokens.shape[1] // 4

    mine = [
        jnp.where(on_gate, gate_packed[:HEAD], up_packed[:HEAD]),
        jnp.where(on_gate, gate_packed[HEAD:], up_packed[HEAD:]),
    ]
    tokens, mine[0] = lax.optimization_barrier((tokens, mine[0]))
    beside = swap(tokens, CORE, CORE)
    first = [swap(mine[0], X, Y)]
    mine[1], first[0] = lax.optimization_barrier((mine[1], first[0]))
    first.append(swap(mine[1], X, Y))
    start = quarter * jnp.where(on_gate, 2 * (1 - y_at) + plane, 2 * plane + 1 - x_at)
    quarters = [lax.dynamic_slice_in_dim(rows, start, quarter, 1) for rows in (tokens, beside)]
    gate_after, up_after, quarters = lax.optimization_barrier(
        (gate_packed, up_packed, jnp.concatenate(quarters))
    )
    direct = swap(quarters, Y, X)
    tokens_after, beside, direct = lax.optimization_barrier((tokens, beside, direct))
    passed = lax.ppermute(direct, "tp", [(i, i ^ 1) for i in range(lax.axis_size("tp"))])
    split = third * BLK
    low = swap(jnp.where(on_gate, up_packed[:, :split], gate_packed[:, :split]), CORE, CORE)
    high = swap(jnp.where(on_gate, up_after[:, split:], gate_after[:, split:]), CORE, CORE)
    far_low = swap(low, X, Y)
    high, passed = lax.optimization_barrier((high, passed))
    far_high = swap(high, X, Y)
    chip = me >> 1
    far_chip = chip ^ jnp.where(on_gate, 1, 2)
    both = jnp.concatenate([tokens_after, beside])
    own = jnp.concatenate(
        [lax.dynamic_slice_in_dim(both, at * quarter, quarter, 1) for at in (chip, far_chip)], axis=1
    )

    early, panel = early_sums(col_slots, (own, direct, passed), (*mine, low, high, *first))
    parts = []
    for n in range(3):
        sources = (far_low,) if n == 0 else (far_low, far_high)
        own, other, near = late_sums(
            n * third // 2, third // 2, col_slots, panel, early, sources
        )
        count = own.shape[0]
        near = near.astype(jnp.float16)
        own = own + swap(near[:count], Y, X).astype(jnp.float32)
        other = swap(other, CORE, CORE) + swap(near[count:], Y | CORE, X | CORE).astype(jnp.float32)
        parts.append((jnp.where(on_gate, own, other), jnp.where(on_gate, other, own)))
    return parts


def shards(
    tokens,
    gate_packed,
    up_packed,
    col_slots,
    readout,
    base_logp,
    ref_logp,
    seq_lengths,
    pair_index,
    noise_flags,
):
    whole = gate_packed.shape[0] % BLK == 0 and col_slots.shape[1] % 3 == 0
    by_core = lax.axis_size("fsdp") == 8 and lax.axis_size("tp") % 2 == 0 and whole
    sums = exchanged_parts if by_core else gathered_parts
    hiddens, contrib, done = [], 0.0, 0
    for gate_sum, up_sum in sums(tokens, gate_packed, up_packed, col_slots):
        hidden = (jax.nn.silu(gate_sum) * up_sum).astype(jnp.bfloat16)
        columns = slice(done, done + hidden.shape[1])
        contrib += jnp.dot(hidden, readout[columns], preferred_element_type=jnp.float32)
        hiddens.append(hidden)
        done = columns.stop
    hidden = jnp.concatenate(hiddens, axis=1)
    local_term = jnp.where(lax.axis_index("tp") == 0, base_logp - ref_logp, jnp.float32(0.0))
    return hidden, pair_losses(local_term + contrib, seq_lengths, pair_index, noise_flags)


def solution(mesh):
    in_specs = (
        P("fsdp", None),
        P("fsdp", "tp"),
        P("fsdp", "tp"),
        P(None, "tp"),
        P("tp"),
        P("fsdp"),
        P("fsdp"),
        P("fsdp", None),
        P("fsdp", None),
        P("fsdp"),
    )
    out_specs = (P("fsdp", "tp"), P("fsdp"))
    return jax.shard_map(shards, mesh=mesh, in_specs=in_specs, out_specs=out_specs, check_vma=False)
```

```python
import functools
import math

import jax
import jax.numpy as jnp
from jax import lax
from jax.experimental import pallas as pl
from jax.experimental.pallas import tpu as pltpu
from jax.sharding import PartitionSpec as P

BLK = 128
EARLY_VMEM, LATE_VMEM = 18 << 20, 12 << 20
HEAD = 3 * BLK // 2
CORE, X, Y = 1, 2, 4


beta_scale = 0.1
smooth_rate = 0.1


def swap(value, core0, core1):
    return lax.ppermute(
        value, "fsdp", [(i, i ^ (core1 if i & CORE else core0)) for i in range(8)]
    )


SMEM, VMEM, ANY = (
    pl.BlockSpec(memory_space=pltpu.SMEM),
    pl.BlockSpec(memory_space=pltpu.VMEM),
    pl.BlockSpec(memory_space=pl.ANY),
)


def places():
    me, plane = lax.axis_index("fsdp"), lax.axis_index("tp") & 1
    core, x_at, y_at = me & 1, (me >> 1) & 1, (me >> 2) & 1
    on_gate = core == 0
    far = me ^ jnp.where(on_gate, X, Y)
    straight = jnp.where(on_gate, x_at, y_at) == plane
    return [me, me ^ CORE, far, far ^ CORE], [straight, straight, ~straight, ~straight]


def find_slots(slot_at, col_slots, block_row, count, at_row):
    for r in range(count):
        for column in range(2 * col_slots.shape[1]):
            slot_at[at_row + r, column] = -1
        for slot in range(col_slots.shape[1]):
            slot_at[at_row + r, col_slots[block_row + r, slot]] = slot


def fill_dense(dense, weights, slot_at, at_row, column):
    for r in range(weights.shape[0] // BLK):
        for h in range(dense.shape[1] // BLK):
            slot = slot_at[at_row + r, column + h]
            at = pl.multiple_of(jnp.maximum(slot, 0) * BLK, BLK)
            block = weights[r * BLK : (r + 1) * BLK, pl.ds(at, BLK)]
            rows = slice((at_row + r) * BLK, (at_row + r + 1) * BLK)
            dense[rows, h * BLK : (h + 1) * BLK] = jnp.where(slot >= 0, block, jnp.zeros_like(block))


def early_kernel(
    col_slots, own, direct, passed, mine1, mine2, low, high, first1, first2,
    total, later, panel, weights, dense, slot_at, sems,
):
    (depth, split), head = low.shape, mine1.shape[0]
    rows = depth // BLK

    @pl.when(pl.program_id(0) == 0)
    def _():
        sources = [
            (mine1, weights.at[0, :head]),
            (mine2, weights.at[0, head:]),
            (low, weights.at[1, :, :split]),
            (high, weights.at[1, :, split:]),
            (first1, weights.at[2, :head]),
            (first2, weights.at[2, head:]),
        ]
        chunks, straight = places()
        count = own.shape[0]
        targets = [panel.at[:, s * depth : (s + 1) * depth] for s in range(3)] + [later]
        for s in range(4):
            at = pl.multiple_of((s // 2 * 2 + (chunks[s] & 1)) * depth, depth)
            sources.append((own.at[:, pl.ds(at, depth)], targets[s].at[:count]))
        copies = [pltpu.make_async_copy(a, b, sems.at[n]) for n, (a, b) in enumerate(sources)]
        for copy in copies:
            copy.start()
        for s in range(4):
            near = pl.ds(pl.multiple_of((chunks[s] & 1) * depth, depth), depth)
            target, sem = targets[s].at[count:], sems.at[len(copies)]

            @pl.when(straight[s])
            def _():
                pltpu.make_async_copy(direct.at[:, near], target, sem).start()

            @pl.when(~straight[s])
            def _():
                pltpu.make_async_copy(passed.at[:, near], target, sem).start()

            copies.append(pltpu.make_async_copy(direct.at[:, near], target, sem))
        for s in range(3):
            find_slots(slot_at, col_slots, chunks[s] * rows, rows, s * rows)
        for copy in copies:
            copy.wait()

    column = dense.shape[1] // BLK * pl.program_id(0)
    for s in range(3):
        fill_dense(dense, weights.at[s], slot_at, s * rows, column)
    total[...] = jnp.dot(panel[...], dense[...], preferred_element_type=jnp.float32)


def early_sums(col_slots, tokens, weights):
    count, depth, width = 2 * tokens[0].shape[0], weights[2].shape[0], weights[0].shape[1]
    columns = 2 * col_slots.shape[1]
    step = 3 * 2 * BLK if columns % 6 == 0 else 2 * BLK
    return pl.pallas_call(
        early_kernel,
        grid=(columns * BLK // step,),
        out_shape=(
            jax.ShapeDtypeStruct((count, columns * BLK), jnp.float32),
            jax.ShapeDtypeStruct((count, depth), jnp.bfloat16),
        ),
        in_specs=[SMEM] + [ANY] * 9,
        out_specs=(pl.BlockSpec((count, step), lambda n: (0, n)), VMEM),
        scratch_shapes=[
            pltpu.VMEM((count, 3 * depth), jnp.bfloat16),
            pltpu.VMEM((3, depth, width), jnp.bfloat16),
            pltpu.VMEM((3 * depth, step), jnp.bfloat16),
            pltpu.SMEM((3 * depth // BLK, columns), jnp.int32),
            pltpu.SemaphoreType.DMA((14,)),
        ],
        compiler_params=pltpu.CompilerParams(vmem_limit_bytes=EARLY_VMEM),
        cost_estimate=pl.CostEstimate(
            flops=2 * count * 3 * depth * columns * BLK,
            bytes_accessed=3 * depth * width * 2 + count * columns * BLK * 4,
            transcendentals=0,
        ),
    )(col_slots, *tokens, *weights)


def late_kernel(first_column, col_slots, panel, early, *refs):
    parts, (mine, beside, near, dense, slot_at) = refs[:-5], refs[-5:]
    rows, lasts = panel.shape[1] // BLK, [part.shape[1] // BLK for part in parts]

    @pl.when(pl.program_id(0) == 0)
    def _():
        find_slots(slot_at, col_slots, places()[0][3] * rows, rows, 0)

    column = first_column + dense.shape[1] // BLK * pl.program_id(0)
    for r in range(rows):
        at_rows = slice(r * BLK, (r + 1) * BLK)
        for h in range(dense.shape[1] // BLK):
            slot = slot_at[r, column + h]
            block, before = jnp.zeros((BLK, BLK), dense.dtype), 0
            for part, count in zip(parts, lasts):
                at = pl.multiple_of(jnp.clip(slot - before, 0, count - 1) * BLK, BLK)
                block = jnp.where(slot >= before, part[at_rows, pl.ds(at, BLK)], block)
                before += count
            dense[at_rows, h * BLK : (h + 1) * BLK] = block
    total = early[...] + jnp.dot(panel[...], dense[...], preferred_element_type=jnp.float32)
    count = mine.shape[0]
    mine[...] = total[:count]
    beside[...] = total[count : 2 * count]
    near[...] = total[2 * count :]


def late_sums(first_pair, pairs, col_slots, panel, early, parts):
    count, depth = panel.shape
    width = sum(part.shape[1] for part in parts)
    out_rows = (count // 4, count // 4, count // 2)
    step = pairs * BLK
    first = 2 * first_pair * BLK // step
    return pl.pallas_call(
        functools.partial(late_kernel, 2 * first_pair),
        grid=(pairs * 2 * BLK // step,),
        out_shape=[
            jax.ShapeDtypeStruct((rows, pairs * 2 * BLK), jnp.float32) for rows in out_rows
        ],
        in_specs=[SMEM, VMEM, pl.BlockSpec((count, step), lambda n: (0, first + n))]
        + [VMEM] * len(parts),
        out_specs=[pl.BlockSpec((rows, step), lambda n: (0, n)) for rows in out_rows],
        scratch_shapes=[
            pltpu.VMEM((depth, step), jnp.bfloat16),
            pltpu.SMEM((depth // BLK, 2 * col_slots.shape[1]), jnp.int32),
        ],
        compiler_params=pltpu.CompilerParams(vmem_limit_bytes=LATE_VMEM),
        cost_estimate=pl.CostEstimate(
            flops=2 * count * depth * pairs * 2 * BLK,
            bytes_accessed=depth * width * 2 + 2 * count * pairs * 2 * BLK * 4,
            transcendentals=0,
        ),
    )(col_slots, panel, early, *parts)


def pair_losses(token_terms, seq_lengths, pair_index, noise_flags):
    lengths = seq_lengths[0]
    seq_ends = jnp.cumsum(lengths)
    seq_starts = seq_ends - lengths
    positions = jnp.arange(token_terms.shape[0], dtype=jnp.int32)
    member = (positions[None, :] >= seq_starts[:, None]) & (positions[None, :] < seq_ends[:, None])
    share = jnp.sum(jnp.where(member, token_terms[None, :], jnp.float32(0.0)), axis=1)
    n_fsdp, n_tp = lax.axis_size("fsdp"), lax.axis_size("tp")
    spread = jnp.broadcast_to(share, (n_fsdp * n_tp, share.shape[0]))
    shares = lax.all_to_all(spread, ("fsdp", "tp"), 0, 0, tiled=True)
    ratios = jnp.sum(shares.reshape(n_fsdp, n_tp, share.shape[0]), axis=1).reshape(-1)
    seq_ids = jnp.arange(ratios.shape[0], dtype=jnp.int32)
    picked = jnp.sum(
        jnp.where(pair_index[:, :, None] == seq_ids, ratios, jnp.float32(0.0)), axis=2
    )
    sign_flip = 1.0 - 2.0 * noise_flags.astype(jnp.float32)
    margin = beta_scale * sign_flip * (picked[:, 0] - picked[:, 1])
    return -(1.0 - smooth_rate) * jax.nn.log_sigmoid(margin) - smooth_rate * jax.nn.log_sigmoid(
        -margin
    )


def gathered_parts(tokens, gate_packed, up_packed, col_slots):
    slot_count, row_count = col_slots.shape[1], col_slots.shape[0]
    column_ids = jnp.arange(2 * slot_count, dtype=jnp.int32)
    place = (col_slots[:, :, None] == column_ids[None, None, :]).astype(jnp.bfloat16)

    def product(packed):
        whole = lax.all_gather(packed, "fsdp", axis=0, tiled=True)
        blocks = whole.reshape(row_count, BLK, slot_count, BLK)
        dense = jnp.einsum("rnjc,rjm->rnmc", blocks, place, preferred_element_type=jnp.bfloat16)
        dense = dense.reshape(row_count * BLK, 2 * slot_count * BLK)
        return jnp.dot(tokens, dense, preferred_element_type=jnp.float32)

    return [(product(gate_packed), product(up_packed))]


def exchanged_parts(tokens, gate_packed, up_packed, col_slots):
    me, plane = lax.axis_index("fsdp"), lax.axis_index("tp") & 1
    core, x_at, y_at = me & 1, (me >> 1) & 1, (me >> 2) & 1
    on_gate = core == 0
    slot_count = col_slots.shape[1]
    third = 2 * slot_count // 3
    quarter = tokens.shape[1] // 4

    mine = [
        jnp.where(on_gate, gate_packed[:HEAD], up_packed[:HEAD]),
        jnp.where(on_gate, gate_packed[HEAD:], up_packed[HEAD:]),
    ]
    tokens, mine[0] = lax.optimization_barrier((tokens, mine[0]))
    beside = swap(tokens, CORE, CORE)
    first = [swap(mine[0], X, Y)]
    mine[1], first[0] = lax.optimization_barrier((mine[1], first[0]))
    first.append(swap(mine[1], X, Y))
    start = quarter * jnp.where(on_gate, 2 * (1 - y_at) + plane, 2 * plane + 1 - x_at)
    quarters = [lax.dynamic_slice_in_dim(rows, start, quarter, 1) for rows in (tokens, beside)]
    gate_after, up_after, quarters = lax.optimization_barrier(
        (gate_packed, up_packed, jnp.concatenate(quarters))
    )
    direct = swap(quarters, Y, X)
    tokens_after, beside, direct = lax.optimization_barrier((tokens, beside, direct))
    passed = lax.ppermute(direct, "tp", [(i, i ^ 1) for i in range(lax.axis_size("tp"))])
    split = third * BLK
    low = swap(jnp.where(on_gate, up_packed[:, :split], gate_packed[:, :split]), CORE, CORE)
    high = swap(jnp.where(on_gate, up_after[:, split:], gate_after[:, split:]), CORE, CORE)
    far_low = swap(low, X, Y)
    high, passed = lax.optimization_barrier((high, passed))
    far_high = swap(high, X, Y)
    chip = me >> 1
    far_chip = chip ^ jnp.where(on_gate, 1, 2)
    both = jnp.concatenate([tokens_after, beside])
    own = jnp.concatenate(
        [lax.dynamic_slice_in_dim(both, at * quarter, quarter, 1) for at in (chip, far_chip)], axis=1
    )

    early, panel = early_sums(col_slots, (own, direct, passed), (*mine, low, high, *first))
    scale = 2.0 ** math.floor(math.log2(65504 / (6 * 0.125 * tokens.shape[1] / 2)))
    parts = []
    for n in range(3):
        sources = (far_low,) if n == 0 else (far_low, far_high)
        own, other, near = late_sums(
            n * third // 2, third // 2, col_slots, panel, early, sources
        )
        count = own.shape[0]
        near = (near * scale).astype(jnp.float16)
        same, cross = swap(near[:count], Y, X), swap(near[count:], Y | CORE, X | CORE)
        own = own + same.astype(jnp.float32) * (1 / scale)
        other = swap(other, CORE, CORE) + cross.astype(jnp.float32) * (1 / scale)
        parts.append((jnp.where(on_gate, own, other), jnp.where(on_gate, other, own)))
    return parts


def shards(
    tokens,
    gate_packed,
    up_packed,
    col_slots,
    readout,
    base_logp,
    ref_logp,
    seq_lengths,
    pair_index,
    noise_flags,
):
    whole = gate_packed.shape[0] % BLK == 0 and col_slots.shape[1] % 3 == 0
    by_core = lax.axis_size("fsdp") == 8 and lax.axis_size("tp") % 2 == 0 and whole
    sums = exchanged_parts if by_core else gathered_parts
    hiddens, contrib, done = [], 0.0, 0
    for gate_sum, up_sum in sums(tokens, gate_packed, up_packed, col_slots):
        hidden = (jax.nn.silu(gate_sum) * up_sum).astype(jnp.bfloat16)
        columns = slice(done, done + hidden.shape[1])
        contrib += jnp.dot(hidden, readout[columns], preferred_element_type=jnp.float32)
        hiddens.append(hidden)
        done = columns.stop
    hidden = jnp.concatenate(hiddens, axis=1)
    local_term = jnp.where(lax.axis_index("tp") == 0, base_logp - ref_logp, jnp.float32(0.0))
    return hidden, pair_losses(local_term + contrib, seq_lengths, pair_index, noise_flags)


def solution(mesh):
    in_specs = (
        P("fsdp", None),
        P("fsdp", "tp"),
        P("fsdp", "tp"),
        P(None, "tp"),
        P("tp"),
        P("fsdp"),
        P("fsdp"),
        P("fsdp", None),
        P("fsdp", None),
        P("fsdp"),
    )
    out_specs = (P("fsdp", "tp"), P("fsdp"))
    return jax.shard_map(shards, mesh=mesh, in_specs=in_specs, out_specs=out_specs, check_vma=False)
```

```python
import functools
import math

import jax
import jax.numpy as jnp
from jax import lax
from jax.experimental import pallas as pl
from jax.experimental.pallas import tpu as pltpu
from jax.sharding import PartitionSpec as P

BLK = 128
EARLY_VMEM, LATE_VMEM = 18 << 20, 12 << 20
HEAD = 3 * BLK // 2
CORE, X, Y = 1, 2, 4


beta_scale = 0.1
smooth_rate = 0.1


def swap(value, core0, core1):
    return lax.ppermute(
        value, "fsdp", [(i, i ^ (core1 if i & CORE else core0)) for i in range(8)]
    )


SMEM, VMEM, ANY = (
    pl.BlockSpec(memory_space=pltpu.SMEM),
    pl.BlockSpec(memory_space=pltpu.VMEM),
    pl.BlockSpec(memory_space=pl.ANY),
)


def places():
    me, plane = lax.axis_index("fsdp"), lax.axis_index("tp") & 1
    core, x_at, y_at = me & 1, (me >> 1) & 1, (me >> 2) & 1
    on_gate = core == 0
    far = me ^ jnp.where(on_gate, X, Y)
    straight = jnp.where(on_gate, x_at, y_at) == plane
    return [me, me ^ CORE, far, far ^ CORE], [straight, straight, ~straight, ~straight]


def find_slots(slot_at, col_slots, block_row, count, at_row):
    for r in range(count):
        for column in range(2 * col_slots.shape[1]):
            slot_at[at_row + r, column] = -1
        for slot in range(col_slots.shape[1]):
            slot_at[at_row + r, col_slots[block_row + r, slot]] = slot


def fill_dense(dense, weights, slot_at, at_row, column):
    for r in range(weights.shape[0] // BLK):
        for h in range(dense.shape[1] // BLK):
            slot = slot_at[at_row + r, column + h]
            at = pl.multiple_of(jnp.maximum(slot, 0) * BLK, BLK)
            block = weights[r * BLK : (r + 1) * BLK, pl.ds(at, BLK)]
            rows = slice((at_row + r) * BLK, (at_row + r + 1) * BLK)
            dense[rows, h * BLK : (h + 1) * BLK] = jnp.where(slot >= 0, block, jnp.zeros_like(block))


def early_kernel(
    col_slots, own, direct, passed, mine1, mine2, low, high, first1, first2,
    total, later, panel, weights, dense, slot_at, sems,
):
    (depth, split), head = low.shape, mine1.shape[0]
    rows = depth // BLK

    @pl.when(pl.program_id(0) == 0)
    def _():
        sources = [
            (mine1, weights.at[0, :head]),
            (mine2, weights.at[0, head:]),
            (low, weights.at[1, :, :split]),
            (high, weights.at[1, :, split:]),
            (first1, weights.at[2, :head]),
            (first2, weights.at[2, head:]),
        ]
        chunks, straight = places()
        count = own.shape[0]
        targets = [panel.at[:, s * depth : (s + 1) * depth] for s in range(3)] + [later]
        for s in range(4):
            at = pl.multiple_of((s // 2 * 2 + (chunks[s] & 1)) * depth, depth)
            sources.append((own.at[:, pl.ds(at, depth)], targets[s].at[:count]))
        copies = [pltpu.make_async_copy(a, b, sems.at[n]) for n, (a, b) in enumerate(sources)]
        for copy in copies:
            copy.start()
        for s in range(4):
            near = pl.ds(pl.multiple_of((chunks[s] & 1) * depth, depth), depth)
            target, sem = targets[s].at[count:], sems.at[len(copies)]

            @pl.when(straight[s])
            def _():
                pltpu.make_async_copy(direct.at[:, near], target, sem).start()

            @pl.when(~straight[s])
            def _():
                pltpu.make_async_copy(passed.at[:, near], target, sem).start()

            copies.append(pltpu.make_async_copy(direct.at[:, near], target, sem))
        for s in range(3):
            find_slots(slot_at, col_slots, chunks[s] * rows, rows, s * rows)
        for copy in copies:
            copy.wait()

    column = dense.shape[1] // BLK * pl.program_id(0)
    for s in range(3):
        fill_dense(dense, weights.at[s], slot_at, s * rows, column)
    total[...] = jnp.dot(panel[...], dense[...], preferred_element_type=jnp.float32)


def early_sums(col_slots, tokens, weights):
    count, depth, width = 2 * tokens[0].shape[0], weights[2].shape[0], weights[0].shape[1]
    columns = 2 * col_slots.shape[1]
    step = 3 * 2 * BLK if columns % 6 == 0 else 2 * BLK
    return pl.pallas_call(
        early_kernel,
        grid=(columns * BLK // step,),
        out_shape=(
            jax.ShapeDtypeStruct((count, columns * BLK), jnp.float32),
            jax.ShapeDtypeStruct((count, depth), jnp.bfloat16),
        ),
        in_specs=[SMEM] + [ANY] * 9,
        out_specs=(pl.BlockSpec((count, step), lambda n: (0, n)), VMEM),
        scratch_shapes=[
            pltpu.VMEM((count, 3 * depth), jnp.bfloat16),
            pltpu.VMEM((3, depth, width), jnp.bfloat16),
            pltpu.VMEM((3 * depth, step), jnp.bfloat16),
            pltpu.SMEM((3 * depth // BLK, columns), jnp.int32),
            pltpu.SemaphoreType.DMA((14,)),
        ],
        compiler_params=pltpu.CompilerParams(vmem_limit_bytes=EARLY_VMEM),
        cost_estimate=pl.CostEstimate(
            flops=2 * count * 3 * depth * columns * BLK,
            bytes_accessed=3 * depth * width * 2 + count * columns * BLK * 4,
            transcendentals=0,
        ),
    )(col_slots, *tokens, *weights)


def late_kernel(first_column, col_slots, panel, early, *refs):
    parts, (mine, beside, near, dense, slot_at) = refs[:-5], refs[-5:]
    rows, lasts = panel.shape[1] // BLK, [part.shape[1] // BLK for part in parts]

    @pl.when(pl.program_id(0) == 0)
    def _():
        find_slots(slot_at, col_slots, places()[0][3] * rows, rows, 0)

    column = first_column + dense.shape[1] // BLK * pl.program_id(0)
    for r in range(rows):
        at_rows = slice(r * BLK, (r + 1) * BLK)
        for h in range(dense.shape[1] // BLK):
            slot = slot_at[r, column + h]
            block, before = jnp.zeros((BLK, BLK), dense.dtype), 0
            for part, count in zip(parts, lasts):
                at = pl.multiple_of(jnp.clip(slot - before, 0, count - 1) * BLK, BLK)
                block = jnp.where(slot >= before, part[at_rows, pl.ds(at, BLK)], block)
                before += count
            dense[at_rows, h * BLK : (h + 1) * BLK] = block
    total = early[...] + jnp.dot(panel[...], dense[...], preferred_element_type=jnp.float32)
    count = mine.shape[0]
    mine[...] = total[:count]
    beside[...] = total[count : 2 * count]
    near[...] = total[2 * count :]


def late_sums(first_pair, pairs, col_slots, panel, early, parts):
    count, depth = panel.shape
    width = sum(part.shape[1] for part in parts)
    out_rows = (count // 4, count // 4, count // 2)
    step = 2 * pairs * BLK
    first = 2 * first_pair * BLK // step
    return pl.pallas_call(
        functools.partial(late_kernel, 2 * first_pair),
        grid=(pairs * 2 * BLK // step,),
        out_shape=[
            jax.ShapeDtypeStruct((rows, pairs * 2 * BLK), jnp.float32) for rows in out_rows
        ],
        in_specs=[SMEM, VMEM, pl.BlockSpec((count, step), lambda n: (0, first + n))]
        + [VMEM] * len(parts),
        out_specs=[pl.BlockSpec((rows, step), lambda n: (0, n)) for rows in out_rows],
        scratch_shapes=[
            pltpu.VMEM((depth, step), jnp.bfloat16),
            pltpu.SMEM((depth // BLK, 2 * col_slots.shape[1]), jnp.int32),
        ],
        compiler_params=pltpu.CompilerParams(vmem_limit_bytes=LATE_VMEM),
        cost_estimate=pl.CostEstimate(
            flops=2 * count * depth * pairs * 2 * BLK,
            bytes_accessed=depth * width * 2 + 2 * count * pairs * 2 * BLK * 4,
            transcendentals=0,
        ),
    )(col_slots, panel, early, *parts)


def pair_losses(token_terms, seq_lengths, pair_index, noise_flags):
    lengths = seq_lengths[0]
    seq_ends = jnp.cumsum(lengths)
    seq_starts = seq_ends - lengths
    positions = jnp.arange(token_terms.shape[0], dtype=jnp.int32)
    member = (positions[None, :] >= seq_starts[:, None]) & (positions[None, :] < seq_ends[:, None])
    share = jnp.sum(jnp.where(member, token_terms[None, :], jnp.float32(0.0)), axis=1)
    n_fsdp, n_tp = lax.axis_size("fsdp"), lax.axis_size("tp")
    spread = jnp.broadcast_to(share, (n_fsdp * n_tp, share.shape[0]))
    shares = lax.all_to_all(spread, ("fsdp", "tp"), 0, 0, tiled=True)
    ratios = jnp.sum(shares.reshape(n_fsdp, n_tp, share.shape[0]), axis=1).reshape(-1)
    seq_ids = jnp.arange(ratios.shape[0], dtype=jnp.int32)
    picked = jnp.sum(
        jnp.where(pair_index[:, :, None] == seq_ids, ratios, jnp.float32(0.0)), axis=2
    )
    sign_flip = 1.0 - 2.0 * noise_flags.astype(jnp.float32)
    margin = beta_scale * sign_flip * (picked[:, 0] - picked[:, 1])
    return -(1.0 - smooth_rate) * jax.nn.log_sigmoid(margin) - smooth_rate * jax.nn.log_sigmoid(
        -margin
    )


def gathered_parts(tokens, gate_packed, up_packed, col_slots):
    slot_count, row_count = col_slots.shape[1], col_slots.shape[0]
    column_ids = jnp.arange(2 * slot_count, dtype=jnp.int32)
    place = (col_slots[:, :, None] == column_ids[None, None, :]).astype(jnp.bfloat16)

    def product(packed):
        whole = lax.all_gather(packed, "fsdp", axis=0, tiled=True)
        blocks = whole.reshape(row_count, BLK, slot_count, BLK)
        dense = jnp.einsum("rnjc,rjm->rnmc", blocks, place, preferred_element_type=jnp.bfloat16)
        dense = dense.reshape(row_count * BLK, 2 * slot_count * BLK)
        return jnp.dot(tokens, dense, preferred_element_type=jnp.float32)

    return [(product(gate_packed), product(up_packed))]


def exchanged_parts(tokens, gate_packed, up_packed, col_slots):
    me, plane = lax.axis_index("fsdp"), lax.axis_index("tp") & 1
    core, x_at, y_at = me & 1, (me >> 1) & 1, (me >> 2) & 1
    on_gate = core == 0
    slot_count = col_slots.shape[1]
    third = 2 * slot_count // 3
    quarter = tokens.shape[1] // 4

    mine = [
        jnp.where(on_gate, gate_packed[:HEAD], up_packed[:HEAD]),
        jnp.where(on_gate, gate_packed[HEAD:], up_packed[HEAD:]),
    ]
    tokens, mine[0] = lax.optimization_barrier((tokens, mine[0]))
    beside = swap(tokens, CORE, CORE)
    first = [swap(mine[0], X, Y)]
    mine[1], first[0] = lax.optimization_barrier((mine[1], first[0]))
    first.append(swap(mine[1], X, Y))
    start = quarter * jnp.where(on_gate, 2 * (1 - y_at) + plane, 2 * plane + 1 - x_at)
    quarters = [lax.dynamic_slice_in_dim(rows, start, quarter, 1) for rows in (tokens, beside)]
    gate_after, up_after, quarters = lax.optimization_barrier(
        (gate_packed, up_packed, jnp.concatenate(quarters))
    )
    direct = swap(quarters, Y, X)
    tokens_after, beside, direct = lax.optimization_barrier((tokens, beside, direct))
    passed = lax.ppermute(direct, "tp", [(i, i ^ 1) for i in range(lax.axis_size("tp"))])
    split = third * BLK
    low = swap(jnp.where(on_gate, up_packed[:, :split], gate_packed[:, :split]), CORE, CORE)
    high = swap(jnp.where(on_gate, up_after[:, split:], gate_after[:, split:]), CORE, CORE)
    far_low = swap(low, X, Y)
    high, passed = lax.optimization_barrier((high, passed))
    far_high = swap(high, X, Y)
    chip = me >> 1
    far_chip = chip ^ jnp.where(on_gate, 1, 2)
    both = jnp.concatenate([tokens_after, beside])
    own = jnp.concatenate(
        [lax.dynamic_slice_in_dim(both, at * quarter, quarter, 1) for at in (chip, far_chip)], axis=1
    )

    early, panel = early_sums(col_slots, (own, direct, passed), (*mine, low, high, *first))
    scale = 2.0 ** math.floor(math.log2(65504 / (6 * 0.125 * tokens.shape[1] / 2)))
    parts = []
    for n in range(3):
        sources = (far_low,) if n == 0 else (far_low, far_high)
        own, other, near = late_sums(
            n * third // 2, third // 2, col_slots, panel, early, sources
        )
        count = own.shape[0]
        near = (near * scale).astype(jnp.float16)
        cross = swap(near[count:], Y | CORE, X | CORE)
        same = swap(near[:count], Y, X)
        own = own + same.astype(jnp.float32) * (1 / scale)
        other = swap(other, CORE, CORE) + cross.astype(jnp.float32) * (1 / scale)
        parts.append((jnp.where(on_gate, own, other), jnp.where(on_gate, other, own)))
    return parts


def shards(
    tokens,
    gate_packed,
    up_packed,
    col_slots,
    readout,
    base_logp,
    ref_logp,
    seq_lengths,
    pair_index,
    noise_flags,
):
    whole = gate_packed.shape[0] % BLK == 0 and col_slots.shape[1] % 3 == 0
    by_core = lax.axis_size("fsdp") == 8 and lax.axis_size("tp") % 2 == 0 and whole
    sums = exchanged_parts if by_core else gathered_parts
    hiddens, contrib, done = [], 0.0, 0
    for gate_sum, up_sum in sums(tokens, gate_packed, up_packed, col_slots):
        hidden = (jax.nn.silu(gate_sum) * up_sum).astype(jnp.bfloat16)
        columns = slice(done, done + hidden.shape[1])
        contrib += jnp.dot(hidden, readout[columns], preferred_element_type=jnp.float32)
        hiddens.append(hidden)
        done = columns.stop
    hidden = jnp.concatenate(hiddens, axis=1)
    local_term = jnp.where(lax.axis_index("tp") == 0, base_logp - ref_logp, jnp.float32(0.0))
    return hidden, pair_losses(local_term + contrib, seq_lengths, pair_index, noise_flags)


def solution(mesh):
    in_specs = (
        P("fsdp", None),
        P("fsdp", "tp"),
        P("fsdp", "tp"),
        P(None, "tp"),
        P("tp"),
        P("fsdp"),
        P("fsdp"),
        P("fsdp", None),
        P("fsdp", None),
        P("fsdp"),
    )
    out_specs = (P("fsdp", "tp"), P("fsdp"))
    return jax.shard_map(shards, mesh=mesh, in_specs=in_specs, out_specs=out_specs, check_vma=False)
```
